256 devices in a mesh: expert: 64 (over x, z, core), dp: 4 (over y).
Axes of the slice: x: 4, y: 4, z: 8, core: 2. Of those that a mesh axis runs over, the one named last changes fastest.
Arguments:
- tokens: bfloat16 [4096, 4096], P(('expert', 'dp')), may hold values from -6 to 6
- routed_expert_index: int32 [4096, 8], P(('expert', 'dp')), may hold values from 0 to 63, all different within a row; in each aligned block of 16 rows (0 to 15, 16 to 31, ...) at most 4 rows name the same one
- routing_weight: float32 [4096, 8], P(('expert', 'dp')), may hold values from 0.05 to 0.25
- token_tenant_index: int32 [4096], P(('expert', 'dp')), may hold values from 0 to 15
- adapter_present: int32 [16, 64], replicated, may hold values 0 or 1
- gate_weight: bfloat16 [64, 4096, 1536], P('expert', None, 'dp'), may hold values from -0.09375 to 0.09375
- up_weight: bfloat16 [64, 4096, 1536], P('expert', None, 'dp'), may hold values from -0.09375 to 0.09375
- down_weight: bfloat16 [64, 1536, 4096], P('expert', 'dp'), may hold values from -0.15625 to 0.15625
- adapter_input_maps: bfloat16 [16, 64, 32, 4096], P('dp', 'expert'), may hold values from -0.09375 to 0.09375
- adapter_output_maps: bfloat16 [16, 64, 32, 1536], P('dp', 'expert'), may hold values from -1.5 to 1.5
Outputs:
- mixed_out: bfloat16 [4096, 4096], P(('expert', 'dp'))
The draws below stay inside these ranges and needn't reach their ends.
Inputs may be any that keep to these rules, and one draw needn't show every extreme that they name: `routed_expert_index`: each row names 8 different experts. In each aligned block of 16 rows (the rows of one device) no expert is named by more than 4 rows, and in every draw some expert is named by exactly 4 rows of some block.
All inputs are finite; a program needn't handle non-finite values.
Results may differ from the reference program's by a relative error of at most 0.015.
Values may be sent and summed in bfloat16 or wider, within the bound.
No kernel may reach another device: no remote copies, remote signals or barrier semaphores. Data moves between devices by JAX's collectives and lax.ppermute only.
A program may use at most 128 MiB of HBM per device.

```python
import math
import jax
import jax.numpy as jnp
import numpy as np
from jax import lax

MODEL_WIDTH = 4096
HIDDEN_UNITS = 1536
TOPK = 8
ADAPTER_RANK = 16
TENANT_COUNT = 16
TOK_DEV = 16
EXPERT_COUNT = 64
CAP = 4
HID_DEV = 384
TOKENS = 4096
N_DP = 4


def plant(array, key, least, high):
    longest = array.shape.index(max(array.shape))
    spots = []
    for shift in (0, 1):
        where = [jax.random.randint(jax.random.fold_in(key, axis), (), 0, length) for axis, length in enumerate(array.shape)]
        where[longest] = (where[longest] + shift) % array.shape[longest]
        spots.append(tuple(where))
    return array.at[spots[0]].set(least).at[spots[1]].set(high)


def level_of(own_key, shape, cuts, smallest, high):
    level = 1.0
    for dim, parts in cuts:
        draws = jax.random.uniform(jax.random.fold_in(jax.random.fold_in(own_key, 6), dim), (parts,), jnp.float32, smallest / len(cuts), high / len(cuts))
        level = level * jnp.repeat(jnp.exp(draws), shape[dim] // parts).reshape((-1,) + (1,) * (len(shape) - 1 - dim))
    return level


def shared_out(rng, own, number, rows, count, top, bound, lean):
    ranking = jax.random.permutation(rng, count)
    packed, usual = portions_of(count, rows * top, bound, lean, True), portions_of(count, rows * top, bound, lean, False)
    places = jnp.arange(count)

    def named(sizes, offset_by):
        used = int((sizes > 0).sum())
        fixed = max(1, used // 4)
        passed = fixed + (places - fixed + offset_by * (used - fixed)) % max(1, count - fixed)
        return jnp.zeros((count,), jnp.int32).at[ranking[jnp.where(places < fixed, places, passed)]].set(jnp.asarray(sizes, jnp.int32))

    sizes = jnp.where(number % 4 == 0, named(packed, number // 4), named(usual, number - number // 4 - 1))
    mixed = jax.random.permutation(jax.random.fold_in(own, 3), count)
    giver, receiver = mixed[0:count // 2 * 2:2], mixed[1:count // 2 * 2:2]
    slack = jnp.minimum(sizes[giver] - 1, bound - sizes[receiver]) // 2
    slack = jnp.where((giver == ranking[0]) | (receiver == ranking[0]) | (sizes[receiver] == 0), 0, jnp.maximum(slack, 0))
    passed = jax.random.randint(jax.random.fold_in(own, 4), (count // 2,), 0, 1 << 20) % (slack + 1)
    sizes = sizes.at[giver].add(-passed).at[receiver].add(passed)
    items = jnp.searchsorted(jnp.cumsum(sizes), jnp.arange(rows * top), side="right").astype(jnp.int32)
    grid = items.reshape(top, rows).T
    grid = grid[jax.random.permutation(jax.random.fold_in(own, 1), rows)]
    offset_by = jax.random.randint(jax.random.fold_in(own, 2), (rows, 1), 0, top)
    return jnp.take_along_axis(grid, (jnp.arange(top)[None, :] + offset_by) % top, axis=1)


def portions_of(amount, total, reach, skew, full):
    loads = [(1 << 20) // math.isqrt(standing ** skew) + 1 for standing in range(1, amount + 1)]
    largest = reach if full else min(reach, max(-(-total // amount), total * loads[0] // sum(loads)))
    least = 1 if total - largest >= amount - 1 else 0
    holding, surplus = [largest] + [least] * (amount - 1), total - largest - least * (amount - 1)
    while surplus > 0:
        candidates = [i for i in range(1, amount) if holding[i] < largest] or [i for i in range(1, amount) if holding[i] < reach]
        pool, budget = sum([loads[i] for i in candidates]), surplus
        for i in candidates:
            addition = min(reach - holding[i], max(1, budget * loads[i] // pool), surplus)
            holding[i] = holding[i] + addition
            surplus = surplus - addition
    return np.array(holding)


def gaussian(key, dims, spread, most, shards=(), kind=jnp.bfloat16):
    values = spread * jax.random.normal(key, dims, jnp.float32)
    if shards:
        values = values * level_of(key, dims, shards, -0.22, 0.18)
    return jnp.clip(values, -most, most).astype(kind)


def setup_inputs(seed: int = 0) -> dict:
    keys = jax.random.split(jax.random.key(seed), 11)
    tokens = gaussian(keys[0], (TOKENS, MODEL_WIDTH), 1.0, 6.0, ((0, 256),))
    routed_expert_index_keys = jax.random.split(jax.random.fold_in(keys[1], 1), TOKENS // TOK_DEV)
    routed_expert_index_turns = jax.random.permutation(jax.random.fold_in(keys[1], 3), TOKENS // TOK_DEV)
    routed_expert_index = jax.vmap(lambda own, number: shared_out(jax.random.fold_in(keys[1], 2), own, number, TOK_DEV, EXPERT_COUNT, TOPK, CAP, 2))(routed_expert_index_keys, routed_expert_index_turns).reshape((TOKENS, TOPK))
    routing_weight = jnp.clip(0.05 + 0.2 * jax.random.uniform(keys[2], (TOKENS, TOPK), jnp.float32) ** level_of(keys[2], (TOKENS, TOPK), ((0, 256),), -0.2, 0.2), 0.05, 0.25)
    token_tenant_index = plant(jax.random.randint(keys[3], (TOKENS,), 0, TENANT_COUNT), jax.random.fold_in(keys[3], 1), 0, TENANT_COUNT - 1).astype(jnp.int32)
    adapter_present = plant((jax.random.randint(keys[4], (TENANT_COUNT, EXPERT_COUNT), 0, 4) < 3).astype(jnp.int32), jax.random.fold_in(keys[4], 1), 0, 1)
    gate_weight = gaussian(keys[5], (EXPERT_COUNT, MODEL_WIDTH, HIDDEN_UNITS), MODEL_WIDTH ** -0.5, 0.09375, ((0, 64), (2, 4)))
    up_weight = gaussian(keys[6], (EXPERT_COUNT, MODEL_WIDTH, HIDDEN_UNITS), MODEL_WIDTH ** -0.5, 0.09375, ((0, 64), (2, 4)))
    down_weight = gaussian(keys[7], (EXPERT_COUNT, HIDDEN_UNITS, MODEL_WIDTH), HIDDEN_UNITS ** -0.5, 0.15625, ((0, 64), (1, 4)))
    adapter_input_maps = gaussian(keys[8], (TENANT_COUNT, EXPERT_COUNT, 2 * ADAPTER_RANK, MODEL_WIDTH), MODEL_WIDTH ** -0.5, 0.09375, ((0, 4), (1, 64)))
    adapter_output_maps = gaussian(keys[9], (TENANT_COUNT, EXPERT_COUNT, 2 * ADAPTER_RANK, HIDDEN_UNITS), ADAPTER_RANK ** -0.5, 1.5, ((0, 4), (1, 64)))
    return {"tokens": tokens, "routed_expert_index": routed_expert_index, "routing_weight": routing_weight, "token_tenant_index": token_tenant_index, "adapter_present": adapter_present, "gate_weight": gate_weight, "up_weight": up_weight, "down_weight": down_weight, "adapter_input_maps": adapter_input_maps, "adapter_output_maps": adapter_output_maps}


def copy_slots(pick_rows):
    flat_ids = pick_rows.reshape(-1)
    matches = (flat_ids[:, None] == jnp.arange(EXPERT_COUNT, dtype=jnp.int32)[None, :]).astype(jnp.int32)
    before = jnp.cumsum(matches, axis=0) - matches
    return flat_ids * CAP + jnp.sum(before * matches, axis=1)


def reference(tokens, routed_expert_index, routing_weight, token_tenant_index, adapter_present, gate_weight, up_weight, down_weight, adapter_input_maps, adapter_output_maps):
    sources = TOKENS // TOK_DEV
    copies = TOK_DEV * TOPK
    slot_ids = jax.vmap(copy_slots)(routed_expert_index.reshape(sources, TOK_DEV, TOPK)).astype(jnp.int32)
    source_idx = jnp.arange(sources, dtype=jnp.int32)[:, None]
    token_idx = (jnp.arange(copies, dtype=jnp.int32) // TOPK)[None, :] + source_idx * TOK_DEV
    token_table = jnp.full((sources, EXPERT_COUNT * CAP), -1, jnp.int32).at[source_idx, slot_ids].set(token_idx.astype(jnp.int32))
    weight_table = jnp.zeros((sources, EXPERT_COUNT * CAP), jnp.float32).at[source_idx, slot_ids].set(routing_weight.reshape(sources, copies).astype(jnp.float32))
    token_table = token_table.reshape(sources, EXPERT_COUNT, CAP)
    weight_table = weight_table.reshape(sources, EXPERT_COUNT, CAP)
    tenant_axis = jnp.arange(TENANT_COUNT, dtype=jnp.int32)

    def one_expert(running, expert_index):
        members = lax.dynamic_index_in_dim(token_table, expert_index, 1, keepdims=False).reshape(-1)
        scaling = lax.dynamic_index_in_dim(weight_table, expert_index, 1, keepdims=False).reshape(-1)
        occupied = members >= 0
        safe_idx = jnp.maximum(members, 0).astype(jnp.int32)
        slot_rows = jnp.where(occupied[:, None], tokens[safe_idx], jnp.zeros((), tokens.dtype))
        tenant_hit = token_tenant_index[safe_idx][:, None] == tenant_axis[None, :]
        live_col = lax.dynamic_index_in_dim(adapter_present, expert_index, 1, keepdims=False)
        chosen = jnp.where(tenant_hit, live_col[None, :].astype(jnp.float32), jnp.zeros((), jnp.float32))
        input_map_block = lax.dynamic_index_in_dim(adapter_input_maps, expert_index, 1, keepdims=False).reshape(TENANT_COUNT * 2 * ADAPTER_RANK, MODEL_WIDTH)
        low_all = jnp.dot(slot_rows, input_map_block.T, preferred_element_type=jnp.float32).reshape(-1, TENANT_COUNT, 2 * ADAPTER_RANK)
        low_rank = jnp.sum(chosen[:, :, None] * low_all, axis=1).astype(jnp.bfloat16)
        onehot = tenant_hit.astype(jnp.bfloat16)
        output_map_block = lax.dynamic_index_in_dim(adapter_output_maps, expert_index, 1, keepdims=False)
        gate_low = (onehot[:, :, None] * low_rank[:, None, :ADAPTER_RANK]).reshape(-1, TENANT_COUNT * ADAPTER_RANK)
        up_low = (onehot[:, :, None] * low_rank[:, None, ADAPTER_RANK:]).reshape(-1, TENANT_COUNT * ADAPTER_RANK)
        gate_act = jnp.dot(slot_rows, gate_weight[expert_index], preferred_element_type=jnp.float32) + jnp.dot(gate_low, output_map_block[:, :ADAPTER_RANK, :].reshape(TENANT_COUNT * ADAPTER_RANK, HIDDEN_UNITS), preferred_element_type=jnp.float32)
        up_act = jnp.dot(slot_rows, up_weight[expert_index], preferred_element_type=jnp.float32) + jnp.dot(up_low, output_map_block[:, ADAPTER_RANK:, :].reshape(TENANT_COUNT * ADAPTER_RANK, HIDDEN_UNITS), preferred_element_type=jnp.float32)
        hidden = (jax.nn.silu(gate_act) * up_act).astype(jnp.bfloat16)
        down_block = down_weight[expert_index]
        result = jnp.zeros((hidden.shape[0], MODEL_WIDTH), jnp.float32)
        for block_idx in range(N_DP):
            low_end = block_idx * HID_DEV
            piece_out = jnp.dot(hidden[:, low_end:low_end + HID_DEV], down_block[low_end:low_end + HID_DEV], preferred_element_type=jnp.float32).astype(jnp.bfloat16)
            result = result + lax.optimization_barrier(piece_out).astype(jnp.float32)
        running = running.at[safe_idx].add(scaling[:, None] * result)
        return running, None

    running, unused = lax.scan(one_expert, jnp.zeros((TOKENS, MODEL_WIDTH), jnp.float32), jnp.arange(EXPERT_COUNT, dtype=jnp.int32))
    return running.astype(jnp.bfloat16)
```

```python
import functools

import jax
import jax.numpy as jnp
from jax import lax
from jax.experimental import pallas as pl
from jax.experimental.pallas import tpu as pltpu
from jax.sharding import PartitionSpec as P

PIECES = 4
SLOTS = 4
BF16 = jnp.bfloat16
F32 = jnp.float32


def over_dp(value, shift):
    size = lax.axis_size("dp")
    return lax.ppermute(value, "dp", [(i, (i + shift) % size) for i in range(size)])


def other_core(value):
    size = lax.axis_size("expert")
    return lax.ppermute(value, "expert", [(i, i ^ 1) for i in range(size)])


def core_major(owners):
    return [list(range(0, owners, 2)) + list(range(1, owners, 2))]


def exchange(rows, owners):
    return lax.all_to_all(
        rows,
        "expert",
        split_axis=0,
        concat_axis=0,
        axis_index_groups=core_major(owners),
        tiled=True,
    )


def accumulate_kernel(first, with_acts, with_low, *refs):
    refs = list(refs)
    blocks = [refs.pop(0) for _ in range(4)]
    if with_acts:
        gate_w, up_w = refs.pop(0), refs.pop(0)
    if with_low:
        maps = refs.pop(0)
    count = 2 * with_acts + with_low
    if not first:
        old, refs = refs[:count], refs[count:]
    new = refs

    @pl.when(pl.program_id(0) == 0)
    def _():
        for i in range(count):
            new[i][...] = jnp.zeros_like(new[i]) if first else old[i][...]

    for b, block in enumerate(blocks):
        rows = block[0]
        height = rows.shape[0]
        span = pl.ds(b * height, height)
        if with_acts:
            new[0][span, :] += jnp.dot(rows, gate_w[0], preferred_element_type=F32)
            new[1][span, :] += jnp.dot(rows, up_w[0], preferred_element_type=F32)
        if with_low:
            new[-1][:, span] += lax.dot_general(
                maps[...], rows, (((1,), (1,)), ((), ())), preferred_element_type=F32
            )


def accumulate(piece, step, blocks, acts, low, gate_weight, up_weight, maps, with_acts, with_low):
    height = blocks[0].shape[1]
    total = 4 * height
    hid = gate_weight.shape[2]
    first = piece == 0
    block_spec = pl.BlockSpec((1, height, step), lambda h: (h, 0, 0))
    weight_spec = pl.BlockSpec((1, step, hid), lambda h: (0, h * PIECES + piece, 0))
    map_spec = pl.BlockSpec((maps.shape[0], step), lambda h: (0, h * PIECES + piece))
    act_spec = pl.BlockSpec((total, hid), lambda h: (0, 0))
    low_spec = pl.BlockSpec((maps.shape[0], total), lambda h: (0, 0))
    operands, specs = list(blocks), [block_spec] * 4
    sums, sum_specs = [], []
    flops = 0
    if with_acts:
        operands += [gate_weight, up_weight]
        specs += [weight_spec] * 2
        sums += [jax.ShapeDtypeStruct((total, hid), F32)] * 2
        sum_specs += [act_spec] * 2
        flops += 2 * total * 2 * step * 2 * hid
    if with_low:
        operands.append(maps)
        specs.append(map_spec)
        sums.append(jax.ShapeDtypeStruct((maps.shape[0], total), F32))
        sum_specs.append(low_spec)
        flops += 2 * total * 2 * step * maps.shape[0]
    aliases = {}
    if not first:
        aliases = {len(operands) + i: i for i in range(len(sums))}
        operands += (list(acts) if with_acts else []) + ([low] if with_low else [])
        specs += sum_specs
    moved = 4 * total * step + sum(2 * 4 * s.shape[0] * s.shape[1] for s in sums)
    return pl.pallas_call(
        functools.partial(accumulate_kernel, first, with_acts, with_low),
        grid=(2,),
        in_specs=specs,
        out_specs=tuple(sum_specs),
        out_shape=tuple(sums),
        input_output_aliases=aliases,
        cost_estimate=pl.CostEstimate(flops=flops, bytes_accessed=moved, transcendentals=0),
        compiler_params=pltpu.CompilerParams(vmem_limit_bytes=40 * 2**20),
    )(*operands)


def hidden_kernel(gate_ref, up_ref, low_ref, tenant_ref, gate_b_ref, up_b_ref, *outs):
    low = low_ref[...]
    half = low.shape[0] // 2
    tenants = gate_b_ref.shape[0] // half
    wide = low.shape[1]
    owner = lax.broadcasted_iota(jnp.int32, (tenants * half, wide), 0) // half
    hit = owner == tenant_ref[...]
    zero = jnp.zeros((), F32)

    def spread(part):
        tall = jnp.concatenate([part] * tenants, axis=0)
        return jnp.where(hit, tall, zero).astype(BF16)

    def product(part, maps):
        return lax.dot_general(
            spread(part), maps, (((0,), (0,)), ((), ())), preferred_element_type=F32
        )

    gate = gate_ref[...] + product(low[:half], gate_b_ref[...])
    up = up_ref[...] + product(low[half:], up_b_ref[...])
    hidden = (gate / (1.0 + jnp.exp(-gate)) * up).astype(BF16)
    height = outs[0].shape[0]
    for i, out in enumerate(outs):
        out[...] = hidden[i * height : (i + 1) * height]


def hidden_blocks(gate, up, low, tenants, gate_b, up_b):
    total, hid = gate.shape
    shape = jax.ShapeDtypeStruct((total // 4, hid), BF16)
    return pl.pallas_call(
        hidden_kernel,
        out_shape=(shape,) * 4,
        cost_estimate=pl.CostEstimate(
            flops=4 * total * hid * gate_b.shape[0], bytes_accessed=9 * total * hid, transcendentals=total * hid
        ),
        compiler_params=pltpu.CompilerParams(vmem_limit_bytes=40 * 2**20),
    )(gate, up, low, tenants, gate_b, up_b)


def down_kernel(count, *refs):
    hidden, weight = refs[0], refs[1]
    total = jnp.dot(hidden[...], weight[0], preferred_element_type=F32)
    for ref in refs[2 : 2 + count]:
        total = total + ref[0].astype(F32)
    refs[2 + count][0] = total.astype(BF16)


def down_block(piece, step, hidden, down_weight, *sums):
    height, hid = hidden.shape
    spec = pl.BlockSpec((1, height, step), lambda h: (h, 0, 0))
    return pl.pallas_call(
        functools.partial(down_kernel, len(sums)),
        grid=(2,),
        in_specs=[
            pl.BlockSpec((height, hid), lambda h: (0, 0)),
            pl.BlockSpec((1, hid, step), lambda h: (0, 0, h * PIECES + piece)),
        ]
        + [spec] * len(sums),
        out_specs=spec,
        out_shape=jax.ShapeDtypeStruct((2, height, step), BF16),
        cost_estimate=pl.CostEstimate(
            flops=4 * height * hid * step,
            bytes_accessed=4 * height * step * (1 + len(sums)) + 4 * hid * step,
            transcendentals=0,
        ),
    )(hidden, down_weight, *sums)


def body(
    tokens,
    routed_expert_index,
    routing_weight,
    token_tenant_index,
    adapter_present,
    gate_weight,
    up_weight,
    down_weight,
    adapter_input_maps,
    adapter_output_maps,
):
    owners = lax.axis_size("expert")
    chips = owners // 2
    tok_dev, width = tokens.shape
    picks = routed_expert_index.shape[1]
    tenants_all, experts = adapter_present.shape
    own_tenants, _, rank_doubled, _ = adapter_input_maps.shape
    hid_dev = gate_weight.shape[2]
    half = width // 2
    step = half // PIECES
    lanes = 128
    owner_idx = lax.axis_index("expert")
    plane = lax.axis_index("dp")
    core = owner_idx % 2

    notes = jnp.concatenate(
        [
            routed_expert_index,
            token_tenant_index[:, None],
            jnp.zeros((tok_dev, lanes - picks - 1), jnp.int32),
        ],
        axis=1,
    ).astype(BF16)
    lower, upper = tokens[:, :half], tokens[:, half:]
    mine = jnp.where(core == 0, lower, upper)
    theirs = jnp.where(core == 0, upper, lower)
    arrived = other_core(jnp.concatenate([notes, theirs], axis=1))
    both_notes = jnp.concatenate([notes, arrived[:, :lanes]], axis=0)
    both = jnp.concatenate([mine, arrived[:, lanes:]], axis=0)
    both_ids = both_notes[:, :picks].astype(jnp.int32)
    both_tenants = both_notes[:, picks]
    other_weight = other_core(routing_weight)
    both_weight = jnp.concatenate([routing_weight, other_weight], axis=0)

    place = jnp.arange(experts, dtype=jnp.int32)
    expert_order = (place % chips) * 2 + place // chips
    named = both_ids[:, :, None] == expert_order[None, None, :]
    member = jnp.any(named, axis=1)
    row = jnp.arange(2 * tok_dev, dtype=jnp.int32)
    earlier = (row[:, None] > row[None, :]) & (row[:, None] // tok_dev == row[None, :] // tok_dev)
    before = jnp.dot(earlier.astype(BF16), member.astype(BF16), preferred_element_type=F32)
    row_core = jnp.where(row < tok_dev, core, 1 - core)
    key = jnp.where(member, before.astype(jnp.int32) + SLOTS * row_core[:, None], -1)
    slot = jnp.arange(2 * SLOTS, dtype=jnp.int32)
    filled = key.T[:, None, :] == slot[None, :, None]
    onehot = filled.reshape(experts * 2 * SLOTS, 2 * tok_dev).astype(BF16)

    height = chips * 2 * SLOTS

    def start_piece(piece):
        part = both[:, piece * step : (piece + 1) * step]
        if piece == 0:
            label = jnp.broadcast_to(both_tenants[:, None], (2 * tok_dev, lanes))
            part = jnp.concatenate([part, label], axis=1)
        rows = jnp.dot(onehot, part, preferred_element_type=F32).astype(BF16)
        got = exchange(rows.reshape(owners, 2 * SLOTS, part.shape[1]), owners)
        return got.reshape(2, height, part.shape[1])

    def spread_piece(piece, own):
        from_left = over_dp(own, 1)
        from_right = over_dp(own, -1)
        if piece % 2 == 0:
            across = over_dp(from_left, 1)
        else:
            across = over_dp(from_right, -1)
        return (own, from_left, from_right, across)

    def map_part(shift):
        at = ((plane + shift) % 4) * hid_dev
        return lax.dynamic_slice_in_dim(adapter_output_maps[:, 0], at, hid_dev, axis=2)

    out_maps = jnp.concatenate(
        [
            map_part(0),
            over_dp(map_part(1), 1),
            over_dp(map_part(-1), -1),
            over_dp(map_part(2), 2),
        ],
        axis=0,
    )
    rank = rank_doubled // 2
    gate_b = out_maps[:, :rank].reshape(tenants_all * rank, hid_dev)
    up_b = out_maps[:, rank:].reshape(tenants_all * rank, hid_dev)

    maps = adapter_input_maps.reshape(own_tenants * rank_doubled, width)
    acts, low = None, None
    label_row = None
    for piece in range(PIECES):
        blocks = spread_piece(piece, start_piece(piece))
        if piece == 0:
            label_row = jnp.concatenate([b[0, :, step] for b in blocks]).astype(jnp.int32)[None, :]
        if piece < PIECES - 1:
            gate, up, low = accumulate(
                piece, step, blocks, acts, low, gate_weight, up_weight, maps, True, True
            )
            acts = (gate, up)
        else:
            (low,) = accumulate(
                piece, step, blocks, acts, low, gate_weight, up_weight, maps, False, True
            )
            acts = accumulate(
                piece, step, blocks, acts, low, gate_weight, up_weight, maps, True, False
            )

    live = lax.dynamic_index_in_dim(adapter_present, owner_idx, axis=1, keepdims=False)
    own_live = lax.dynamic_slice_in_dim(live, plane * own_tenants, own_tenants)
    own_ids = plane * own_tenants + jnp.arange(own_tenants, dtype=jnp.int32)
    chosen = (label_row == own_ids[:, None]) & (own_live[:, None] != 0)
    low_own = jnp.sum(
        jnp.where(chosen[:, None, :], low.reshape(own_tenants, rank_doubled, 4 * height), 0.0),
        axis=0,
    ).astype(BF16)
    quarters = [low_own[:, i * height : (i + 1) * height] for i in range(4)]

    def arranged(order):
        return jnp.concatenate([quarters[i] for i in order], axis=1)

    low_rank = (
        low_own.astype(F32)
        + over_dp(arranged((2, 0, 3, 1)), 1).astype(F32)
        + over_dp(arranged((1, 3, 0, 2)), -1).astype(F32)
        + over_dp(arranged((3, 2, 1, 0)), 2).astype(F32)
    )
    away = (label_row // own_tenants - plane) % 4
    group = jnp.where(away == 0, 0, jnp.where(away == 3, 1, away + 1))
    label_rel = group * own_tenants + label_row % own_tenants
    hidden = hidden_blocks(acts[0], acts[1], low_rank, label_rel, gate_b, up_b)

    scale = jnp.sum(jnp.where(named, both_weight[:, :, None], 0.0), axis=1)
    mix = jnp.where(filled, scale.T[:, None, :], 0.0).reshape(experts * 2 * SLOTS, 2 * tok_dev)
    mix_hi = lax.optimization_barrier(mix.astype(BF16))
    mix_lo = (mix - mix_hi.astype(F32)).astype(BF16)

    def return_piece(piece):
        if piece % 2 == 0:
            relay, through, direct, ahead = 1, 2, 1, -1
        else:
            relay, through, direct, ahead = -1, 1, 2, 1
        down = functools.partial(down_block, piece, step)
        relayed = over_dp(down(hidden[3], down_weight), relay)
        near = over_dp(down(hidden[direct], down_weight), ahead)
        far = over_dp(down(hidden[through], down_weight, relayed), relay)
        total = down(hidden[0], down_weight, near, far)
        back = exchange(total.reshape(owners, 2 * SLOTS, step), owners)
        back = back.reshape(owners * 2 * SLOTS, step)
        contract = (((0,), (0,)), ((), ()))
        return (
            lax.dot_general(mix_hi, back, contract, preferred_element_type=F32)
            + lax.dot_general(mix_lo, back, contract, preferred_element_type=F32)
        ).astype(BF16)

    mixed = jnp.concatenate([return_piece(piece) for piece in range(PIECES)], axis=1)
    kept, sent = mixed[:tok_dev], mixed[tok_dev:]
    came = other_core(sent)
    return jnp.where(
        core == 0,
        jnp.concatenate([kept, came], axis=1),
        jnp.concatenate([came, kept], axis=1),
    )


def solution(mesh):
    placed = (
        P(("expert", "dp"), None),
        P(("expert", "dp"), None),
        P(("expert", "dp"), None),
        P(("expert", "dp")),
        P(),
        P("expert", None, "dp"),
        P("expert", None, "dp"),
        P("expert", "dp", None),
        P("dp", "expert", None, None),
        P("dp", "expert", None, None),
    )
    return jax.shard_map(
        body, mesh=mesh, in_specs=placed, out_specs=P(("expert", "dp"), None), check_vma=False
    )
```

```python
import functools

import jax
import jax.numpy as jnp
from jax import lax
from jax.experimental import pallas as pl
from jax.experimental.pallas import tpu as pltpu
from jax.sharding import PartitionSpec as P

PIECES = 2
LANES = 128
TILE = 1024
SLOTS = 4
BF16 = jnp.bfloat16
F32 = jnp.float32


def over_dp(value, shift):
    size = lax.axis_size("dp")
    return lax.ppermute(value, "dp", [(i, (i + shift) % size) for i in range(size)])


def other_core(value):
    size = lax.axis_size("expert")
    return lax.ppermute(value, "expert", [(i, i ^ 1) for i in range(size)])


def core_major(owners):
    return [list(range(0, owners, 2)) + list(range(1, owners, 2))]


def exchange(rows, owners):
    return lax.all_to_all(
        rows,
        "expert",
        split_axis=0,
        concat_axis=0,
        axis_index_groups=core_major(owners),
        tiled=True,
    )


def accumulate_kernel(first, near, with_acts, with_low, unread, *refs):
    refs = list(refs)[unread:]
    blocks = [refs.pop(0) for _ in range(3 if near else 2)]
    if with_acts:
        gate_w, up_w = refs.pop(0), refs.pop(0)
    if with_low:
        maps = refs.pop(0)
    count = 2 * with_acts + with_low
    if first:
        notes = [refs.pop(0) for _ in range(3 if near else 1)]
        label = refs.pop()
    else:
        old, refs = refs[:count], refs[count:]
    new = refs
    h = pl.program_id(0)

    @pl.when(h == 0)
    def _():
        for i in range(count):
            new[i][...] = jnp.zeros_like(new[i]) if first else old[i][...]
        if first:
            at = (lax.broadcasted_iota(jnp.int32, (8, LANES), 1) == 0).astype(BF16)
            for b, note in enumerate(notes):
                height = note.shape[1]
                label[:, pl.ds(b * height, height)] = lax.dot_general(
                    at, note[0], (((1,), (1,)), ((), ())), preferred_element_type=F32
                )

    def add(b, rows):
        height = rows.shape[0]
        span = pl.ds(b * height, height)
        if with_acts:
            new[0][span, :] += jnp.dot(rows, gate_w[0], preferred_element_type=F32)
            new[1][span, :] += jnp.dot(rows, up_w[0], preferred_element_type=F32)
        if with_low:
            new[-1][:, span] += lax.dot_general(
                maps[...], rows, (((1,), (1,)), ((), ())), preferred_element_type=F32
            )

    if near:
        for b, block in enumerate(blocks):
            add(b, block[0])
    else:
        add(0, jnp.where(h == 0, blocks[0][0], blocks[1][0]))


def accumulate(
    piece, step, near, blocks, sums, gate_weight, up_weight, maps, with_acts, with_low, after=()
):
    height = blocks[0].shape[1]
    total = (3 if near else 1) * height
    hid = gate_weight.shape[2]
    first = piece == 0
    if near:
        block_spec = pl.BlockSpec((1, height, step), lambda h: (h, 0, 0))
    else:
        block_spec = pl.BlockSpec((1, height, step), lambda h: (0, 0, 0))
    weight_spec = pl.BlockSpec((1, step, hid), lambda h: (0, h * PIECES + piece, 0))
    map_spec = pl.BlockSpec((maps.shape[0], step), lambda h: (0, h * PIECES + piece))
    operands, specs = [*after, *blocks], [block_spec] * len(blocks)
    specs = [pl.BlockSpec(memory_space=pl.ANY)] * len(after) + specs
    shapes = []
    flops = 0
    if with_acts:
        operands += [gate_weight, up_weight]
        specs += [weight_spec] * 2
        shapes += [(total, hid)] * 2
        flops += 2 * total * 2 * step * 2 * hid
    if with_low:
        operands.append(maps)
        specs.append(map_spec)
        shapes.append((maps.shape[0], total))
        flops += 2 * total * 2 * step * maps.shape[0]
    sum_specs = [pl.BlockSpec(shape, lambda h: (0, 0)) for shape in shapes]
    aliases = {}
    if first:
        noted = blocks if near else blocks[:1]
        operands += noted
        specs += [pl.BlockSpec((1, height, LANES), lambda h: (0, 0, step // LANES))] * len(noted)
        shapes.append((8, total))
        sum_specs.append(pl.BlockSpec((8, total), lambda h: (0, 0)))
    else:
        aliases = {len(operands) + i: i for i in range(len(shapes))}
        operands += list(sums)
        specs += sum_specs
    moved = 4 * total * step + sum(2 * 4 * a * b for a, b in shapes)
    return pl.pallas_call(
        functools.partial(accumulate_kernel, first, near, with_acts, with_low, len(after)),
        grid=(2,),
        in_specs=specs,
        out_specs=tuple(sum_specs),
        out_shape=tuple(jax.ShapeDtypeStruct(shape, F32) for shape in shapes),
        input_output_aliases=aliases,
        cost_estimate=pl.CostEstimate(flops=flops, bytes_accessed=moved, transcendentals=0),
        compiler_params=pltpu.CompilerParams(vmem_limit_bytes=40 * 2**20),
    )(*operands)


def hidden_kernel(gate_ref, up_ref, low_ref, tenant_ref, gate_b_ref, up_b_ref, *outs):
    low = low_ref[...]
    half = low.shape[0] // 2
    tenants = gate_b_ref.shape[0] // half
    wide = low.shape[1]
    owner = lax.broadcasted_iota(jnp.int32, (tenants * half, wide), 0) // half
    hit = owner == tenant_ref[...]
    zero = jnp.zeros((), F32)

    def spread(part):
        tall = jnp.concatenate([part] * tenants, axis=0)
        return jnp.where(hit, tall, zero).astype(BF16)

    def product(part, maps):
        return lax.dot_general(
            spread(part), maps, (((0,), (0,)), ((), ())), preferred_element_type=F32
        )

    gate = gate_ref[...] + product(low[:half], gate_b_ref[...])
    up = up_ref[...] + product(low[half:], up_b_ref[...])
    hidden = (gate / (1.0 + jnp.exp(-gate)) * up).astype(BF16)
    height = outs[0].shape[0]
    for i, out in enumerate(outs):
        out[...] = hidden[i * height : (i + 1) * height]


def hidden_blocks(count, gate, up, low, tenants, gate_b, up_b):
    total, hid = gate.shape
    shape = jax.ShapeDtypeStruct((total // count, hid), BF16)
    return pl.pallas_call(
        hidden_kernel,
        out_shape=(shape,) * count,
        cost_estimate=pl.CostEstimate(
            flops=4 * total * hid * gate_b.shape[0], bytes_accessed=9 * total * hid, transcendentals=total * hid
        ),
        compiler_params=pltpu.CompilerParams(vmem_limit_bytes=40 * 2**20),
    )(gate, up, low, tenants, gate_b, up_b)


def product(hidden, weight):
    return jnp.dot(hidden[...], weight[0], preferred_element_type=F32)


def down_cost(blocks, height, hid, step):
    return pl.CostEstimate(
        flops=4 * blocks * height * hid * step,
        bytes_accessed=6 * blocks * height * step + 4 * hid * step,
        transcendentals=0,
    )


def weight_tile(piece, step, hid):
    tiles = step // TILE
    return pl.BlockSpec(
        (1, hid, TILE), lambda h, t: (0, 0, h * PIECES * tiles + piece * tiles + t)
    )


def rows_kernel(onehot, part, after, out):
    out[...] = jnp.dot(onehot[...], part[...], preferred_element_type=F32).astype(BF16)


def build_rows(onehot, part, after):
    count, columns = onehot.shape[0], part.shape[1]
    whole = pl.BlockSpec(memory_space=pltpu.VMEM)
    return pl.pallas_call(
        rows_kernel,
        in_specs=[whole, whole, pl.BlockSpec(memory_space=pl.ANY)],
        out_specs=whole,
        out_shape=jax.ShapeDtypeStruct((count, columns), BF16),
        cost_estimate=pl.CostEstimate(
            flops=64 * count * columns, bytes_accessed=2 * count * columns, transcendentals=0
        ),
    )(onehot, part, after)


def split_kernel(left, right, *refs):
    refs[-2][...] = left[...]
    refs[-1][...] = right[...]


def split_halves(left, right, after):
    _, height, columns = left.shape
    shape = jax.ShapeDtypeStruct((1, height, columns), left.dtype)
    block = pl.BlockSpec((1, height, columns), lambda h: (0, 0, 0))
    return pl.pallas_call(
        split_kernel,
        grid=(1,),
        in_specs=[block, pl.BlockSpec((1, height, columns), lambda h: (1, 0, 0))]
        + [pl.BlockSpec(memory_space=pl.ANY)] * len(after),
        out_specs=(block, block),
        out_shape=(shape, shape),
        cost_estimate=pl.CostEstimate(
            flops=1, bytes_accessed=8 * height * columns, transcendentals=0
        ),
    )(left, right, *after)


def relay_kernel(hidden, weight, lower, upper):
    total = product(hidden, weight).astype(BF16)

    @pl.when(pl.program_id(0) == 0)
    def _():
        lower[...] = total

    @pl.when(pl.program_id(0) == 1)
    def _():
        upper[...] = total


def relay_blocks(piece, step, hidden, down_weight):
    height, hid = hidden.shape
    last = step // TILE - 1
    shape = jax.ShapeDtypeStruct((height, step), BF16)
    return pl.pallas_call(
        relay_kernel,
        grid=(2, step // TILE),
        in_specs=[
            pl.BlockSpec((height, hid), lambda h, t: (0, 0)),
            weight_tile(piece, step, hid),
        ],
        out_specs=(
            pl.BlockSpec((height, TILE), lambda h, t: (0, jnp.where(h == 0, t, last))),
            pl.BlockSpec((height, TILE), lambda h, t: (0, jnp.where(h == 0, 0, t))),
        ),
        out_shape=(shape, shape),
        cost_estimate=down_cost(1, height, hid, step),
    )(hidden, down_weight)


def pass_kernel(up_hidden, down_hidden, weight, lower, upper, up_out, down_out):
    h = pl.program_id(0)
    zero = jnp.zeros((), F32)
    up = product(up_hidden, weight) + jnp.where(h == 0, lower[...].astype(F32), zero)
    down = product(down_hidden, weight) + jnp.where(h == 1, upper[...].astype(F32), zero)
    up_out[0] = up.astype(BF16)
    down_out[0] = down.astype(BF16)


def pass_blocks(piece, step, up_hidden, down_hidden, down_weight, lower, upper):
    height, hid = up_hidden.shape
    whole = pl.BlockSpec((height, hid), lambda h, t: (0, 0))
    part = pl.BlockSpec((height, TILE), lambda h, t: (0, t))
    out = pl.BlockSpec((1, height, TILE), lambda h, t: (h, 0, t))
    shape = jax.ShapeDtypeStruct((2, height, step), BF16)
    return pl.pallas_call(
        pass_kernel,
        grid=(2, step // TILE),
        in_specs=[whole, whole, weight_tile(piece, step, hid), part, part],
        out_specs=(out, out),
        out_shape=(shape, shape),
        cost_estimate=down_cost(2, height, hid, step),
    )(up_hidden, down_hidden, down_weight, lower, upper)


def last_kernel(hidden, weight, left, right, *refs):
    total = product(hidden, weight) + left[0].astype(F32) + right[0].astype(F32)
    refs[-1][0] = total.astype(BF16)


def last_block(piece, step, hidden, down_weight, left, right, after):
    height, hid = hidden.shape
    block = pl.BlockSpec((1, height, TILE), lambda h, t: (h, 0, t))
    return pl.pallas_call(
        last_kernel,
        grid=(2, step // TILE),
        in_specs=[
            pl.BlockSpec((height, hid), lambda h, t: (0, 0)),
            weight_tile(piece, step, hid),
            block,
            block,
        ]
        + [pl.BlockSpec(memory_space=pl.ANY)] * len(after),
        out_specs=block,
        out_shape=jax.ShapeDtypeStruct((2, height, step), BF16),
        cost_estimate=down_cost(1, height, hid, step),
    )(hidden, down_weight, left, right, *after)


def body(
    tokens,
    routed_expert_index,
    routing_weight,
    token_tenant_index,
    adapter_present,
    gate_weight,
    up_weight,
    down_weight,
    adapter_input_maps,
    adapter_output_maps,
):
    owners = lax.axis_size("expert")
    chips = owners // 2
    tok_dev, width = tokens.shape
    picks = routed_expert_index.shape[1]
    tenants_all, experts = adapter_present.shape
    own_tenants, _, rank_doubled, _ = adapter_input_maps.shape
    hid_dev = gate_weight.shape[2]
    half = width // 2
    step = half // PIECES
    lanes = 128
    owner_idx = lax.axis_index("expert")
    plane = lax.axis_index("dp")
    core = owner_idx % 2

    notes = jnp.concatenate(
        [
            routed_expert_index,
            token_tenant_index[:, None],
            jnp.zeros((tok_dev, lanes - picks - 1), jnp.int32),
        ],
        axis=1,
    ).astype(BF16)
    lower, upper = tokens[:, :half], tokens[:, half:]
    mine = jnp.where(core == 0, lower, upper)
    theirs = jnp.where(core == 0, upper, lower)
    arrived = other_core(jnp.concatenate([notes, theirs], axis=1))
    both_notes = jnp.concatenate([notes, arrived[:, :lanes]], axis=0)
    both = jnp.concatenate([mine, arrived[:, lanes:]], axis=0)
    both_ids = both_notes[:, :picks].astype(jnp.int32)
    both_tenants = both_notes[:, picks]
    other_weight = other_core(routing_weight)
    both_weight = jnp.concatenate([routing_weight, other_weight], axis=0)

    place = jnp.arange(experts, dtype=jnp.int32)
    expert_order = (place % chips) * 2 + place // chips
    named = both_ids[:, :, None] == expert_order[None, None, :]
    member = jnp.any(named, axis=1)
    row = jnp.arange(2 * tok_dev, dtype=jnp.int32)
    earlier = (row[:, None] > row[None, :]) & (row[:, None] // tok_dev == row[None, :] // tok_dev)
    before = jnp.dot(earlier.astype(BF16), member.astype(BF16), preferred_element_type=F32)
    row_core = jnp.where(row < tok_dev, core, 1 - core)
    key = jnp.where(member, before.astype(jnp.int32) + SLOTS * row_core[:, None], -1)
    slot = jnp.arange(2 * SLOTS, dtype=jnp.int32)
    filled = key.T[:, None, :] == slot[None, :, None]
    onehot = filled.reshape(experts * 2 * SLOTS, 2 * tok_dev).astype(BF16)

    height = chips * 2 * SLOTS

    def start_piece(piece, after):
        part = both[:, piece * step : (piece + 1) * step]
        if piece == 0:
            label = jnp.broadcast_to(both_tenants[:, None], (2 * tok_dev, lanes))
            part = jnp.concatenate([part, label], axis=1)
        rows = build_rows(onehot, part, after)
        got = exchange(rows.reshape(owners, 2 * SLOTS, part.shape[1]), owners)
        return got.reshape(2, height, part.shape[1])

    def spread_piece(own, after):
        from_left = over_dp(own, 1)
        from_right = over_dp(own, -1)
        lower, upper = split_halves(from_left, from_right, after)
        across = (over_dp(lower, 1), over_dp(upper, -1))
        return (own, from_left, from_right), across, (lower, upper)

    def map_part(shift):
        at = ((plane + shift) % 4) * hid_dev
        return lax.dynamic_slice_in_dim(adapter_output_maps[:, 0], at, hid_dev, axis=2)

    out_maps = jnp.concatenate(
        [
            map_part(0),
            over_dp(map_part(1), 1),
            over_dp(map_part(-1), -1),
            over_dp(map_part(2), 2),
        ],
        axis=0,
    )
    rank = rank_doubled // 2
    gate_b = out_maps[:, :rank].reshape(tenants_all * rank, hid_dev)
    up_b = out_maps[:, rank:].reshape(tenants_all * rank, hid_dev)

    maps = adapter_input_maps.reshape(own_tenants * rank_doubled, width)
    near_sums, far_sums, far = (), (), ()
    for piece in range(PIECES):
        near, far, halves = spread_piece(start_piece(piece, notes if piece == 0 else out_maps), far)
        run = functools.partial(accumulate, piece, step)
        shared = (gate_weight, up_weight, maps)
        if piece == 0:
            *near_sums, near_label = run(True, near, near_sums, *shared, True, True, after=halves)
            *far_sums, far_label = run(False, far, far_sums, *shared, True, True)
        elif piece < PIECES - 1:
            near_sums = run(True, near, near_sums, *shared, True, True, after=halves)
            far_sums = run(False, far, far_sums, *shared, True, True)
        else:
            near_sums = run(True, near, near_sums, *shared, True, True, after=halves)
            (far_low,) = run(False, far, far_sums[2:], *shared, False, True)
            far_acts = run(False, far, far_sums[:2], *shared, True, False)
    label_row = jnp.concatenate([near_label[:1], far_label[:1]], axis=1).astype(jnp.int32)
    low = jnp.concatenate([near_sums[2], far_low], axis=1)

    live = lax.dynamic_index_in_dim(adapter_present, owner_idx, axis=1, keepdims=False)
    own_live = lax.dynamic_slice_in_dim(live, plane * own_tenants, own_tenants)
    own_ids = plane * own_tenants + jnp.arange(own_tenants, dtype=jnp.int32)
    chosen = (label_row == own_ids[:, None]) & (own_live[:, None] != 0)
    low_own = jnp.sum(
        jnp.where(chosen[:, None, :], low.reshape(own_tenants, rank_doubled, 4 * height), 0.0),
        axis=0,
    ).astype(BF16)
    quarters = [low_own[:, i * height : (i + 1) * height] for i in range(4)]

    def arranged(order):
        return jnp.concatenate([quarters[i] for i in order], axis=1)

    low_rank = (
        low_own.astype(F32)
        + over_dp(arranged((2, 0, 3, 1)), 1).astype(F32)
        + over_dp(arranged((1, 3, 0, 2)), -1).astype(F32)
        + over_dp(arranged((3, 2, 1, 0)), 2).astype(F32)
    )
    away = (label_row // own_tenants - plane) % 4
    group = jnp.where(away == 0, 0, jnp.where(away == 3, 1, away + 1))
    label_rel = group * own_tenants + label_row % own_tenants
    split = 3 * height
    hidden_far = hidden_blocks(
        1, *far_acts, low_rank[:, split:], label_rel[:, split:], gate_b, up_b
    )
    hidden_near = hidden_blocks(
        3, *near_sums[:2], low_rank[:, :split], label_rel[:, :split], gate_b, up_b
    )

    scale = jnp.sum(jnp.where(named, both_weight[:, :, None], 0.0), axis=1)
    mix = jnp.where(filled, scale.T[:, None, :], 0.0).reshape(experts * 2 * SLOTS, 2 * tok_dev)
    mix_hi = lax.optimization_barrier(mix.astype(BF16))
    mix_lo = (mix - mix_hi.astype(F32)).astype(BF16)

    relays = [relay_blocks(piece, step, hidden_far[0], down_weight) for piece in range(PIECES)]
    relayed = [(over_dp(lower, 1), over_dp(upper, -1)) for lower, upper in relays]
    passed = [
        pass_blocks(piece, step, hidden_near[2], hidden_near[1], down_weight, *relayed[piece])
        for piece in range(PIECES)
    ]

    def return_piece(piece):
        up_sum, down_sum = passed[piece]
        after = relayed[piece + 1] if piece + 1 < PIECES else ()
        total = last_block(
            piece, step, hidden_near[0], down_weight, over_dp(up_sum, 1), over_dp(down_sum, -1), after
        )
        back = exchange(total.reshape(owners, 2 * SLOTS, step), owners)
        back = back.reshape(owners * 2 * SLOTS, step)
        contract = (((0,), (0,)), ((), ()))
        return (
            lax.dot_general(mix_hi, back, contract, preferred_element_type=F32)
            + lax.dot_general(mix_lo, back, contract, preferred_element_type=F32)
        ).astype(BF16)

    mixed = jnp.concatenate([return_piece(piece) for piece in range(PIECES)], axis=1)
    kept, sent = mixed[:tok_dev], mixed[tok_dev:]
    came = other_core(sent)
    return jnp.where(
        core == 0,
        jnp.concatenate([kept, came], axis=1),
        jnp.concatenate([came, kept], axis=1),
    )


def solution(mesh):
    placed = (
        P(("expert", "dp"), None),
        P(("expert", "dp"), None),
        P(("expert", "dp"), None),
        P(("expert", "dp")),
        P(),
        P("expert", None, "dp"),
        P("expert", None, "dp"),
        P("expert", "dp", None),
        P("dp", "expert", None, None),
        P("dp", "expert", None, None),
    )
    return jax.shard_map(
        body, mesh=mesh, in_specs=placed, out_specs=P(("expert", "dp"), None), check_vma=False
    )
```

```python
import functools

import jax
import jax.numpy as jnp
from jax import lax
from jax.experimental import pallas as pl
from jax.experimental.pallas import tpu as pltpu
from jax.sharding import PartitionSpec as P

PIECES = 2
LANES = 128
TILE = 1024
SLOTS = 4
BF16 = jnp.bfloat16
F32 = jnp.float32


def over_dp(value, shift):
    size = lax.axis_size("dp")
    return lax.ppermute(value, "dp", [(i, (i + shift) % size) for i in range(size)])


def other_core(value):
    size = lax.axis_size("expert")
    return lax.ppermute(value, "expert", [(i, i ^ 1) for i in range(size)])


def core_major(owners):
    return [list(range(0, owners, 2)) + list(range(1, owners, 2))]


def exchange(rows, owners):
    return lax.all_to_all(
        rows,
        "expert",
        split_axis=0,
        concat_axis=0,
        axis_index_groups=core_major(owners),
        tiled=True,
    )


def accumulate_kernel(first, near, with_acts, with_low, *refs):
    refs = list(refs)
    blocks = [refs.pop(0) for _ in range(3 if near else 2)]
    if with_acts:
        gate_w, up_w = refs.pop(0), refs.pop(0)
    if with_low:
        maps = refs.pop(0)
    count = 2 * with_acts + with_low
    if first:
        notes = [refs.pop(0) for _ in range(3 if near else 1)]
        label = refs.pop()
    else:
        old, refs = refs[:count], refs[count:]
    new = refs
    h = pl.program_id(0)

    @pl.when(h == 0)
    def _():
        for i in range(count):
            new[i][...] = jnp.zeros_like(new[i]) if first else old[i][...]
        if first:
            at = (lax.broadcasted_iota(jnp.int32, (8, LANES), 1) == 0).astype(BF16)
            for b, note in enumerate(notes):
                height = note.shape[1]
                label[:, pl.ds(b * height, height)] = lax.dot_general(
                    at, note[0], (((1,), (1,)), ((), ())), preferred_element_type=F32
                )

    def add(b, rows):
        height = rows.shape[0]
        span = pl.ds(b * height, height)
        if with_acts:
            new[0][span, :] += jnp.dot(rows, gate_w[0], preferred_element_type=F32)
            new[1][span, :] += jnp.dot(rows, up_w[0], preferred_element_type=F32)
        if with_low:
            new[-1][:, span] += lax.dot_general(
                maps[...], rows, (((1,), (1,)), ((), ())), preferred_element_type=F32
            )

    if near:
        for b, block in enumerate(blocks):
            add(b, block[0])
    else:
        add(0, jnp.where(h == 0, blocks[0][0], blocks[1][0]))


def accumulate(piece, step, near, blocks, sums, gate_weight, up_weight, maps, with_acts, with_low):
    height = blocks[0].shape[1]
    total = (3 if near else 1) * height
    hid = gate_weight.shape[2]
    first = piece == 0
    if near:
        block_spec = pl.BlockSpec((1, height, step), lambda h: (h, 0, 0))
    else:
        block_spec = pl.BlockSpec((1, height, step), lambda h: (0, 0, 0))
    weight_spec = pl.BlockSpec((1, step, hid), lambda h: (0, h * PIECES + piece, 0))
    map_spec = pl.BlockSpec((maps.shape[0], step), lambda h: (0, h * PIECES + piece))
    operands, specs = list(blocks), [block_spec] * len(blocks)
    shapes = []
    flops = 0
    if with_acts:
        operands += [gate_weight, up_weight]
        specs += [weight_spec] * 2
        shapes += [(total, hid)] * 2
        flops += 2 * total * 2 * step * 2 * hid
    if with_low:
        operands.append(maps)
        specs.append(map_spec)
        shapes.append((maps.shape[0], total))
        flops += 2 * total * 2 * step * maps.shape[0]
    sum_specs = [pl.BlockSpec(shape, lambda h: (0, 0)) for shape in shapes]
    aliases = {}
    if first:
        noted = blocks if near else blocks[:1]
        operands += noted
        specs += [pl.BlockSpec((1, height, LANES), lambda h: (0, 0, step // LANES))] * len(noted)
        shapes.append((8, total))
        sum_specs.append(pl.BlockSpec((8, total), lambda h: (0, 0)))
    else:
        aliases = {len(operands) + i: i for i in range(len(shapes))}
        operands += list(sums)
        specs += sum_specs
    moved = 4 * total * step + sum(2 * 4 * a * b for a, b in shapes)
    return pl.pallas_call(
        functools.partial(accumulate_kernel, first, near, with_acts, with_low),
        grid=(2,),
        in_specs=specs,
        out_specs=tuple(sum_specs),
        out_shape=tuple(jax.ShapeDtypeStruct(shape, F32) for shape in shapes),
        input_output_aliases=aliases,
        cost_estimate=pl.CostEstimate(flops=flops, bytes_accessed=moved, transcendentals=0),
        compiler_params=pltpu.CompilerParams(vmem_limit_bytes=40 * 2**20),
    )(*operands)


def hidden_kernel(gate_ref, up_ref, low_ref, tenant_ref, gate_b_ref, up_b_ref, *outs):
    low = low_ref[...]
    half = low.shape[0] // 2
    tenants = gate_b_ref.shape[0] // half
    wide = low.shape[1]
    owner = lax.broadcasted_iota(jnp.int32, (tenants * half, wide), 0) // half
    hit = owner == tenant_ref[...]
    zero = jnp.zeros((), F32)

    def spread(part):
        tall = jnp.concatenate([part] * tenants, axis=0)
        return jnp.where(hit, tall, zero).astype(BF16)

    def product(part, maps):
        return lax.dot_general(
            spread(part), maps, (((0,), (0,)), ((), ())), preferred_element_type=F32
        )

    gate = gate_ref[...] + product(low[:half], gate_b_ref[...])
    up = up_ref[...] + product(low[half:], up_b_ref[...])
    hidden = (gate / (1.0 + jnp.exp(-gate)) * up).astype(BF16)
    height = outs[0].shape[0]
    for i, out in enumerate(outs):
        out[...] = hidden[i * height : (i + 1) * height]


def hidden_blocks(count, gate, up, low, tenants, gate_b, up_b):
    total, hid = gate.shape
    shape = jax.ShapeDtypeStruct((total // count, hid), BF16)
    return pl.pallas_call(
        hidden_kernel,
        out_shape=(shape,) * count,
        cost_estimate=pl.CostEstimate(
            flops=4 * total * hid * gate_b.shape[0], bytes_accessed=9 * total * hid, transcendentals=total * hid
        ),
        compiler_params=pltpu.CompilerParams(vmem_limit_bytes=40 * 2**20),
    )(gate, up, low, tenants, gate_b, up_b)


def product(hidden, weight):
    return jnp.dot(hidden[...], weight[0], preferred_element_type=F32)


def down_cost(blocks, height, hid, step):
    return pl.CostEstimate(
        flops=4 * blocks * height * hid * step,
        bytes_accessed=6 * blocks * height * step + 4 * hid * step,
        transcendentals=0,
    )


def weight_tile(piece, step, hid):
    tiles = step // TILE
    return pl.BlockSpec(
        (1, hid, TILE), lambda h, t: (0, 0, h * PIECES * tiles + piece * tiles + t)
    )


def rows_kernel(onehot, part, after, out):
    out[...] = jnp.dot(onehot[...], part[...], preferred_element_type=F32).astype(BF16)


def build_rows(onehot, part, after):
    count, columns = onehot.shape[0], part.shape[1]
    whole = pl.BlockSpec(memory_space=pltpu.VMEM)
    return pl.pallas_call(
        rows_kernel,
        in_specs=[whole, whole, pl.BlockSpec(memory_space=pl.ANY)],
        out_specs=whole,
        out_shape=jax.ShapeDtypeStruct((count, columns), BF16),
        cost_estimate=pl.CostEstimate(
            flops=64 * count * columns, bytes_accessed=2 * count * columns, transcendentals=0
        ),
    )(onehot, part, after)


def split_kernel(left, right, *refs):
    refs[-2][...] = left[...]
    refs[-1][...] = right[...]


def split_halves(left, right, after):
    _, height, columns = left.shape
    shape = jax.ShapeDtypeStruct((1, height, columns), left.dtype)
    block = pl.BlockSpec((1, height, columns), lambda h: (0, 0, 0))
    return pl.pallas_call(
        split_kernel,
        grid=(1,),
        in_specs=[block, pl.BlockSpec((1, height, columns), lambda h: (1, 0, 0))]
        + [pl.BlockSpec(memory_space=pl.ANY)] * len(after),
        out_specs=(block, block),
        out_shape=(shape, shape),
        cost_estimate=pl.CostEstimate(
            flops=1, bytes_accessed=8 * height * columns, transcendentals=0
        ),
    )(left, right, *after)


def relay_kernel(hidden, weight, lower, upper):
    total = product(hidden, weight).astype(BF16)

    @pl.when(pl.program_id(0) == 0)
    def _():
        lower[...] = total

    @pl.when(pl.program_id(0) == 1)
    def _():
        upper[...] = total


def relay_blocks(piece, step, hidden, down_weight):
    height, hid = hidden.shape
    last = step // TILE - 1
    shape = jax.ShapeDtypeStruct((height, step), BF16)
    return pl.pallas_call(
        relay_kernel,
        grid=(2, step // TILE),
        in_specs=[
            pl.BlockSpec((height, hid), lambda h, t: (0, 0)),
            weight_tile(piece, step, hid),
        ],
        out_specs=(
            pl.BlockSpec((height, TILE), lambda h, t: (0, jnp.where(h == 0, t, last))),
            pl.BlockSpec((height, TILE), lambda h, t: (0, jnp.where(h == 0, 0, t))),
        ),
        out_shape=(shape, shape),
        cost_estimate=down_cost(1, height, hid, step),
    )(hidden, down_weight)


def pass_kernel(up_hidden, down_hidden, weight, lower, upper, up_out, down_out):
    h = pl.program_id(0)
    zero = jnp.zeros((), F32)
    up = product(up_hidden, weight) + jnp.where(h == 0, lower[...].astype(F32), zero)
    down = product(down_hidden, weight) + jnp.where(h == 1, upper[...].astype(F32), zero)
    up_out[0] = up.astype(BF16)
    down_out[0] = down.astype(BF16)


def pass_blocks(piece, step, up_hidden, down_hidden, down_weight, lower, upper):
    height, hid = up_hidden.shape
    whole = pl.BlockSpec((height, hid), lambda h, t: (0, 0))
    part = pl.BlockSpec((height, TILE), lambda h, t: (0, t))
    out = pl.BlockSpec((1, height, TILE), lambda h, t: (h, 0, t))
    shape = jax.ShapeDtypeStruct((2, height, step), BF16)
    return pl.pallas_call(
        pass_kernel,
        grid=(2, step // TILE),
        in_specs=[whole, whole, weight_tile(piece, step, hid), part, part],
        out_specs=(out, out),
        out_shape=(shape, shape),
        cost_estimate=down_cost(2, height, hid, step),
    )(up_hidden, down_hidden, down_weight, lower, upper)


def last_kernel(hidden, weight, left, right, *refs):
    total = product(hidden, weight) + left[0].astype(F32) + right[0].astype(F32)
    refs[-1][0] = total.astype(BF16)


def last_block(piece, step, hidden, down_weight, left, right, after):
    height, hid = hidden.shape
    block = pl.BlockSpec((1, height, TILE), lambda h, t: (h, 0, t))
    return pl.pallas_call(
        last_kernel,
        grid=(2, step // TILE),
        in_specs=[
            pl.BlockSpec((height, hid), lambda h, t: (0, 0)),
            weight_tile(piece, step, hid),
            block,
            block,
        ]
        + [pl.BlockSpec(memory_space=pl.ANY)] * len(after),
        out_specs=block,
        out_shape=jax.ShapeDtypeStruct((2, height, step), BF16),
        cost_estimate=down_cost(1, height, hid, step),
    )(hidden, down_weight, left, right, *after)


def body(
    tokens,
    routed_expert_index,
    routing_weight,
    token_tenant_index,
    adapter_present,
    gate_weight,
    up_weight,
    down_weight,
    adapter_input_maps,
    adapter_output_maps,
):
    owners = lax.axis_size("expert")
    chips = owners // 2
    tok_dev, width = tokens.shape
    picks = routed_expert_index.shape[1]
    tenants_all, experts = adapter_present.shape
    own_tenants, _, rank_doubled, _ = adapter_input_maps.shape
    hid_dev = gate_weight.shape[2]
    half = width // 2
    step = half // PIECES
    lanes = 128
    owner_idx = lax.axis_index("expert")
    plane = lax.axis_index("dp")
    core = owner_idx % 2

    notes = jnp.concatenate(
        [
            routed_expert_index,
            token_tenant_index[:, None],
            jnp.zeros((tok_dev, lanes - picks - 1), jnp.int32),
        ],
        axis=1,
    ).astype(BF16)
    lower, upper = tokens[:, :half], tokens[:, half:]
    mine = jnp.where(core == 0, lower, upper)
    theirs = jnp.where(core == 0, upper, lower)
    arrived = other_core(jnp.concatenate([notes, theirs], axis=1))
    both_notes = jnp.concatenate([notes, arrived[:, :lanes]], axis=0)
    both = jnp.concatenate([mine, arrived[:, lanes:]], axis=0)
    both_ids = both_notes[:, :picks].astype(jnp.int32)
    both_tenants = both_notes[:, picks]
    other_weight = other_core(routing_weight)
    both_weight = jnp.concatenate([routing_weight, other_weight], axis=0)

    place = jnp.arange(experts, dtype=jnp.int32)
    expert_order = (place % chips) * 2 + place // chips
    named = both_ids[:, :, None] == expert_order[None, None, :]
    member = jnp.any(named, axis=1)
    row = jnp.arange(2 * tok_dev, dtype=jnp.int32)
    earlier = (row[:, None] > row[None, :]) & (row[:, None] // tok_dev == row[None, :] // tok_dev)
    before = jnp.dot(earlier.astype(BF16), member.astype(BF16), preferred_element_type=F32)
    row_core = jnp.where(row < tok_dev, core, 1 - core)
    key = jnp.where(member, before.astype(jnp.int32) + SLOTS * row_core[:, None], -1)
    slot = jnp.arange(2 * SLOTS, dtype=jnp.int32)
    filled = key.T[:, None, :] == slot[None, :, None]
    onehot = filled.reshape(experts * 2 * SLOTS, 2 * tok_dev).astype(BF16)

    height = chips * 2 * SLOTS

    def start_piece(piece, after):
        part = both[:, piece * step : (piece + 1) * step]
        if piece == 0:
            label = jnp.broadcast_to(both_tenants[:, None], (2 * tok_dev, lanes))
            part = jnp.concatenate([part, label], axis=1)
        rows = build_rows(onehot, part, after)
        got = exchange(rows.reshape(owners, 2 * SLOTS, part.shape[1]), owners)
        return got.reshape(2, height, part.shape[1])

    def spread_piece(own, after):
        from_left = over_dp(own, 1)
        from_right = over_dp(own, -1)
        lower, upper = split_halves(from_left, from_right, after)
        across = (over_dp(lower, 1), over_dp(upper, -1))
        return (own, from_left, from_right), across

    def map_part(shift):
        at = ((plane + shift) % 4) * hid_dev
        return lax.dynamic_slice_in_dim(adapter_output_maps[:, 0], at, hid_dev, axis=2)

    out_maps = jnp.concatenate(
        [
            map_part(0),
            over_dp(map_part(1), 1),
            over_dp(map_part(-1), -1),
            over_dp(map_part(2), 2),
        ],
        axis=0,
    )
    rank = rank_doubled // 2
    gate_b = out_maps[:, :rank].reshape(tenants_all * rank, hid_dev)
    up_b = out_maps[:, rank:].reshape(tenants_all * rank, hid_dev)

    maps = adapter_input_maps.reshape(own_tenants * rank_doubled, width)
    near_sums, far_sums, far = (), (), ()
    for piece in range(PIECES):
        near, far = spread_piece(start_piece(piece, notes if piece == 0 else out_maps), far)
        run = functools.partial(accumulate, piece, step)
        shared = (gate_weight, up_weight, maps)
        if piece == 0:
            *near_sums, near_label = run(True, near, near_sums, *shared, True, True)
            *far_sums, far_label = run(False, far, far_sums, *shared, True, True)
        elif piece < PIECES - 1:
            near_sums = run(True, near, near_sums, *shared, True, True)
            far_sums = run(False, far, far_sums, *shared, True, True)
        else:
            near_sums = run(True, near, near_sums, *shared, True, True)
            (far_low,) = run(False, far, far_sums[2:], *shared, False, True)
            far_acts = run(False, far, far_sums[:2], *shared, True, False)
    label_row = jnp.concatenate([near_label[:1], far_label[:1]], axis=1).astype(jnp.int32)
    low = jnp.concatenate([near_sums[2], far_low], axis=1)

    live = lax.dynamic_index_in_dim(adapter_present, owner_idx, axis=1, keepdims=False)
    own_live = lax.dynamic_slice_in_dim(live, plane * own_tenants, own_tenants)
    own_ids = plane * own_tenants + jnp.arange(own_tenants, dtype=jnp.int32)
    chosen = (label_row == own_ids[:, None]) & (own_live[:, None] != 0)
    low_own = jnp.sum(
        jnp.where(chosen[:, None, :], low.reshape(own_tenants, rank_doubled, 4 * height), 0.0),
        axis=0,
    ).astype(BF16)
    quarters = [low_own[:, i * height : (i + 1) * height] for i in range(4)]

    def arranged(order):
        return jnp.concatenate([quarters[i] for i in order], axis=1)

    low_rank = (
        low_own.astype(F32)
        + over_dp(arranged((2, 0, 3, 1)), 1).astype(F32)
        + over_dp(arranged((1, 3, 0, 2)), -1).astype(F32)
        + over_dp(arranged((3, 2, 1, 0)), 2).astype(F32)
    )
    away = (label_row // own_tenants - plane) % 4
    group = jnp.where(away == 0, 0, jnp.where(away == 3, 1, away + 1))
    label_rel = group * own_tenants + label_row % own_tenants
    split = 3 * height
    hidden_far = hidden_blocks(
        1, *far_acts, low_rank[:, split:], label_rel[:, split:], gate_b, up_b
    )
    hidden_near = hidden_blocks(
        3, *near_sums[:2], low_rank[:, :split], label_rel[:, :split], gate_b, up_b
    )

    scale = jnp.sum(jnp.where(named, both_weight[:, :, None], 0.0), axis=1)
    mix = jnp.where(filled, scale.T[:, None, :], 0.0).reshape(experts * 2 * SLOTS, 2 * tok_dev)
    mix_hi = lax.optimization_barrier(mix.astype(BF16))
    mix_lo = (mix - mix_hi.astype(F32)).astype(BF16)

    relays = [relay_blocks(piece, step, hidden_far[0], down_weight) for piece in range(PIECES)]
    relayed = [(over_dp(lower, 1), over_dp(upper, -1)) for lower, upper in relays]
    passed = [
        pass_blocks(piece, step, hidden_near[2], hidden_near[1], down_weight, *relayed[piece])
        for piece in range(PIECES)
    ]

    def return_piece(piece):
        up_sum, down_sum = passed[piece]
        after = relayed[piece + 1] if piece + 1 < PIECES else ()
        total = last_block(
            piece, step, hidden_near[0], down_weight, over_dp(up_sum, 1), over_dp(down_sum, -1), after
        )
        back = exchange(total.reshape(owners, 2 * SLOTS, step), owners)
        back = back.reshape(owners * 2 * SLOTS, step)
        contract = (((0,), (0,)), ((), ()))
        return (
            lax.dot_general(mix_hi, back, contract, preferred_element_type=F32)
            + lax.dot_general(mix_lo, back, contract, preferred_element_type=F32)
        ).astype(BF16)

    mixed = jnp.concatenate([return_piece(piece) for piece in range(PIECES)], axis=1)
    kept, sent = mixed[:tok_dev], mixed[tok_dev:]
    came = other_core(sent)
    return jnp.where(
        core == 0,
        jnp.concatenate([kept, came], axis=1),
        jnp.concatenate([came, kept], axis=1),
    )


def solution(mesh):
    placed = (
        P(("expert", "dp"), None),
        P(("expert", "dp"), None),
        P(("expert", "dp"), None),
        P(("expert", "dp")),
        P(),
        P("expert", None, "dp"),
        P("expert", None, "dp"),
        P("expert", "dp", None),
        P("dp", "expert", None, None),
        P("dp", "expert", None, None),
    )
    return jax.shard_map(
        body, mesh=mesh, in_specs=placed, out_specs=P(("expert", "dp"), None), check_vma=False
    )
```

```python
import functools

import jax
import jax.numpy as jnp
from jax import lax
from jax.experimental import pallas as pl
from jax.experimental.pallas import tpu as pltpu
from jax.sharding import PartitionSpec as P

PIECES = 2
LANES = 128
TILE = 1024
SLOTS = 4
BF16 = jnp.bfloat16
F32 = jnp.float32


def over_dp(value, shift):
    size = lax.axis_size("dp")
    return lax.ppermute(value, "dp", [(i, (i + shift) % size) for i in range(size)])


def other_core(value):
    size = lax.axis_size("expert")
    return lax.ppermute(value, "expert", [(i, i ^ 1) for i in range(size)])


def core_major(owners):
    return [list(range(0, owners, 2)) + list(range(1, owners, 2))]


def exchange(rows, owners):
    return lax.all_to_all(
        rows,
        "expert",
        split_axis=0,
        concat_axis=0,
        axis_index_groups=core_major(owners),
        tiled=True,
    )


def accumulate_kernel(first, near, with_acts, with_low, unread, *refs):
    refs = list(refs)[unread:]
    blocks = [refs.pop(0) for _ in range(3 if near else 2)]
    if with_acts:
        gate_w, up_w = refs.pop(0), refs.pop(0)
    if with_low:
        maps = refs.pop(0)
    count = 2 * with_acts + with_low
    if first:
        notes = [refs.pop(0) for _ in range(3 if near else 1)]
        label = refs.pop()
    else:
        old, refs = refs[:count], refs[count:]
    new = refs
    h = pl.program_id(0)

    @pl.when(h == 0)
    def _():
        for i in range(count):
            new[i][...] = jnp.zeros_like(new[i]) if first else old[i][...]
        if first:
            at = (lax.broadcasted_iota(jnp.int32, (8, LANES), 1) == 0).astype(BF16)
            for b, note in enumerate(notes):
                height = note.shape[1]
                label[:, pl.ds(b * height, height)] = lax.dot_general(
                    at, note[0], (((1,), (1,)), ((), ())), preferred_element_type=F32
                )

    def add(b, rows):
        height = rows.shape[0]
        span = pl.ds(b * height, height)
        if with_acts:
            new[0][span, :] += jnp.dot(rows, gate_w[0], preferred_element_type=F32)
            new[1][span, :] += jnp.dot(rows, up_w[0], preferred_element_type=F32)
        if with_low:
            new[-1][:, span] += lax.dot_general(
                maps[...], rows, (((1,), (1,)), ((), ())), preferred_element_type=F32
            )

    if near:
        for b, block in enumerate(blocks):
            add(b, block[0])
    else:
        add(0, jnp.where(h == 0, blocks[0][0], blocks[1][0]))


def accumulate(
    piece, step, near, blocks, sums, gate_weight, up_weight, maps, with_acts, with_low, after=()
):
    height = blocks[0].shape[1]
    total = (3 if near else 1) * height
    hid = gate_weight.shape[2]
    first = piece == 0
    if near:
        block_spec = pl.BlockSpec((1, height, step), lambda h: (h, 0, 0))
    else:
        block_spec = pl.BlockSpec((1, height, step), lambda h: (0, 0, 0))
    weight_spec = pl.BlockSpec((1, step, hid), lambda h: (0, h * PIECES + piece, 0))
    map_spec = pl.BlockSpec((maps.shape[0], step), lambda h: (0, h * PIECES + piece))
    operands, specs = [*after, *blocks], [block_spec] * len(blocks)
    specs = [pl.BlockSpec(memory_space=pl.ANY)] * len(after) + specs
    shapes = []
    flops = 0
    if with_acts:
        operands += [gate_weight, up_weight]
        specs += [weight_spec] * 2
        shapes += [(total, hid)] * 2
        flops += 2 * total * 2 * step * 2 * hid
    if with_low:
        operands.append(maps)
        specs.append(map_spec)
        shapes.append((maps.shape[0], total))
        flops += 2 * total * 2 * step * maps.shape[0]
    sum_specs = [pl.BlockSpec(shape, lambda h: (0, 0)) for shape in shapes]
    aliases = {}
    if first:
        noted = blocks if near else blocks[:1]
        operands += noted
        specs += [pl.BlockSpec((1, height, LANES), lambda h: (0, 0, step // LANES))] * len(noted)
        shapes.append((8, total))
        sum_specs.append(pl.BlockSpec((8, total), lambda h: (0, 0)))
    else:
        aliases = {len(operands) + i: i for i in range(len(shapes))}
        operands += list(sums)
        specs += sum_specs
    moved = 4 * total * step + sum(2 * 4 * a * b for a, b in shapes)
    return pl.pallas_call(
        functools.partial(accumulate_kernel, first, near, with_acts, with_low, len(after)),
        grid=(2,),
        in_specs=specs,
        out_specs=tuple(sum_specs),
        out_shape=tuple(jax.ShapeDtypeStruct(shape, F32) for shape in shapes),
        input_output_aliases=aliases,
        cost_estimate=pl.CostEstimate(flops=flops, bytes_accessed=moved, transcendentals=0),
        compiler_params=pltpu.CompilerParams(vmem_limit_bytes=40 * 2**20),
    )(*operands)


def hidden_kernel(gate_ref, up_ref, low_ref, tenant_ref, gate_b_ref, up_b_ref, *outs):
    low = low_ref[...]
    half = low.shape[0] // 2
    tenants = gate_b_ref.shape[0] // half
    wide = low.shape[1]
    owner = lax.broadcasted_iota(jnp.int32, (tenants * half, wide), 0) // half
    hit = owner == tenant_ref[...]
    zero = jnp.zeros((), F32)

    def spread(part):
        tall = jnp.concatenate([part] * tenants, axis=0)
        return jnp.where(hit, tall, zero).astype(BF16)

    def product(part, maps):
        return lax.dot_general(
            spread(part), maps, (((0,), (0,)), ((), ())), preferred_element_type=F32
        )

    gate = gate_ref[...] + product(low[:half], gate_b_ref[...])
    up = up_ref[...] + product(low[half:], up_b_ref[...])
    hidden = (gate / (1.0 + jnp.exp(-gate)) * up).astype(BF16)
    height = outs[0].shape[0]
    for i, out in enumerate(outs):
        out[...] = hidden[i * height : (i + 1) * height]


def hidden_blocks(count, gate, up, low, tenants, gate_b, up_b):
    total, hid = gate.shape
    shape = jax.ShapeDtypeStruct((total // count, hid), BF16)
    return pl.pallas_call(
        hidden_kernel,
        out_shape=(shape,) * count,
        cost_estimate=pl.CostEstimate(
            flops=4 * total * hid * gate_b.shape[0], bytes_accessed=9 * total * hid, transcendentals=total * hid
        ),
        compiler_params=pltpu.CompilerParams(vmem_limit_bytes=40 * 2**20),
    )(gate, up, low, tenants, gate_b, up_b)


def product(hidden, weight):
    return jnp.dot(hidden[...], weight[0], preferred_element_type=F32)


def down_cost(blocks, height, hid, step):
    return pl.CostEstimate(
        flops=4 * blocks * height * hid * step,
        bytes_accessed=6 * blocks * height * step + 4 * hid * step,
        transcendentals=0,
    )


def weight_tile(piece, step, hid):
    tiles = step // TILE
    return pl.BlockSpec(
        (1, hid, TILE), lambda h, t: (0, 0, h * PIECES * tiles + piece * tiles + t)
    )


def rows_kernel(onehot, part, after, out):
    out[...] = jnp.dot(onehot[...], part[...], preferred_element_type=F32).astype(BF16)


def build_rows(onehot, part, after):
    count, columns = onehot.shape[0], part.shape[1]
    whole = pl.BlockSpec(memory_space=pltpu.VMEM)
    return pl.pallas_call(
        rows_kernel,
        in_specs=[whole, whole, pl.BlockSpec(memory_space=pl.ANY)],
        out_specs=whole,
        out_shape=jax.ShapeDtypeStruct((count, columns), BF16),
        cost_estimate=pl.CostEstimate(
            flops=64 * count * columns, bytes_accessed=2 * count * columns, transcendentals=0
        ),
    )(onehot, part, after)


def split_kernel(left, right, *refs):
    refs[-2][...] = left[...]
    refs[-1][...] = right[...]


def split_halves(left, right, after):
    _, height, columns = left.shape
    shape = jax.ShapeDtypeStruct((1, height, columns), left.dtype)
    block = pl.BlockSpec((1, height, columns), lambda h: (0, 0, 0))
    return pl.pallas_call(
        split_kernel,
        grid=(1,),
        in_specs=[block, pl.BlockSpec((1, height, columns), lambda h: (1, 0, 0))]
        + [pl.BlockSpec(memory_space=pl.ANY)] * len(after),
        out_specs=(block, block),
        out_shape=(shape, shape),
        cost_estimate=pl.CostEstimate(
            flops=1, bytes_accessed=8 * height * columns, transcendentals=0
        ),
    )(left, right, *after)


def relay_kernel(hidden, weight, lower, upper):
    total = product(hidden, weight).astype(BF16)

    @pl.when(pl.program_id(0) == 0)
    def _():
        lower[...] = total

    @pl.when(pl.program_id(0) == 1)
    def _():
        upper[...] = total


def relay_blocks(piece, step, hidden, down_weight):
    height, hid = hidden.shape
    last = step // TILE - 1
    shape = jax.ShapeDtypeStruct((height, step), BF16)
    return pl.pallas_call(
        relay_kernel,
        grid=(2, step // TILE),
        in_specs=[
            pl.BlockSpec((height, hid), lambda h, t: (0, 0)),
            weight_tile(piece, step, hid),
        ],
        out_specs=(
            pl.BlockSpec((height, TILE), lambda h, t: (0, jnp.where(h == 0, t, last))),
            pl.BlockSpec((height, TILE), lambda h, t: (0, jnp.where(h == 0, 0, t))),
        ),
        out_shape=(shape, shape),
        cost_estimate=down_cost(1, height, hid, step),
    )(hidden, down_weight)


def pass_kernel(up_hidden, down_hidden, weight, lower, upper, up_out, down_out):
    h = pl.program_id(0)
    zero = jnp.zeros((), F32)
    up = product(up_hidden, weight) + jnp.where(h == 0, lower[...].astype(F32), zero)
    down = product(down_hidden, weight) + jnp.where(h == 1, upper[...].astype(F32), zero)
    up_out[0] = up.astype(BF16)
    down_out[0] = down.astype(BF16)


def pass_blocks(piece, step, up_hidden, down_hidden, down_weight, lower, upper):
    height, hid = up_hidden.shape
    whole = pl.BlockSpec((height, hid), lambda h, t: (0, 0))
    part = pl.BlockSpec((height, TILE), lambda h, t: (0, t))
    out = pl.BlockSpec((1, height, TILE), lambda h, t: (h, 0, t))
    shape = jax.ShapeDtypeStruct((2, height, step), BF16)
    return pl.pallas_call(
        pass_kernel,
        grid=(2, step // TILE),
        in_specs=[whole, whole, weight_tile(piece, step, hid), part, part],
        out_specs=(out, out),
        out_shape=(shape, shape),
        cost_estimate=down_cost(2, height, hid, step),
    )(up_hidden, down_hidden, down_weight, lower, upper)


def last_kernel(hidden, weight, left, right, *refs):
    total = product(hidden, weight) + left[0].astype(F32) + right[0].astype(F32)
    refs[-1][0] = total.astype(BF16)


def last_block(piece, step, hidden, down_weight, left, right, after):
    height, hid = hidden.shape
    block = pl.BlockSpec((1, height, TILE), lambda h, t: (h, 0, t))
    return pl.pallas_call(
        last_kernel,
        grid=(2, step // TILE),
        in_specs=[
            pl.BlockSpec((height, hid), lambda h, t: (0, 0)),
            weight_tile(piece, step, hid),
            block,
            block,
        ]
        + [pl.BlockSpec(memory_space=pl.ANY)] * len(after),
        out_specs=block,
        out_shape=jax.ShapeDtypeStruct((2, height, step), BF16),
        cost_estimate=down_cost(1, height, hid, step),
    )(hidden, down_weight, left, right, *after)


def body(
    tokens,
    routed_expert_index,
    routing_weight,
    token_tenant_index,
    adapter_present,
    gate_weight,
    up_weight,
    down_weight,
    adapter_input_maps,
    adapter_output_maps,
):
    owners = lax.axis_size("expert")
    chips = owners // 2
    tok_dev, width = tokens.shape
    picks = routed_expert_index.shape[1]
    tenants_all, experts = adapter_present.shape
    own_tenants, _, rank_doubled, _ = adapter_input_maps.shape
    hid_dev = gate_weight.shape[2]
    half = width // 2
    step = half // PIECES
    lanes = 128
    owner_idx = lax.axis_index("expert")
    plane = lax.axis_index("dp")
    core = owner_idx % 2

    notes = jnp.concatenate(
        [
            routed_expert_index,
            token_tenant_index[:, None],
            jnp.zeros((tok_dev, lanes - picks - 1), jnp.int32),
        ],
        axis=1,
    ).astype(BF16)
    lower, upper = tokens[:, :half], tokens[:, half:]
    mine = jnp.where(core == 0, lower, upper)
    theirs = jnp.where(core == 0, upper, lower)
    arrived = other_core(jnp.concatenate([notes, theirs], axis=1))
    both_notes = jnp.concatenate([notes, arrived[:, :lanes]], axis=0)
    both = jnp.concatenate([mine, arrived[:, lanes:]], axis=0)
    both_ids = both_notes[:, :picks].astype(jnp.int32)
    both_tenants = both_notes[:, picks]
    other_weight = other_core(routing_weight)
    both_weight = jnp.concatenate([routing_weight, other_weight], axis=0)

    place = jnp.arange(experts, dtype=jnp.int32)
    expert_order = (place % chips) * 2 + place // chips
    named = both_ids[:, :, None] == expert_order[None, None, :]
    member = jnp.any(named, axis=1)
    row = jnp.arange(2 * tok_dev, dtype=jnp.int32)
    earlier = (row[:, None] > row[None, :]) & (row[:, None] // tok_dev == row[None, :] // tok_dev)
    before = jnp.dot(earlier.astype(BF16), member.astype(BF16), preferred_element_type=F32)
    row_core = jnp.where(row < tok_dev, core, 1 - core)
    key = jnp.where(member, before.astype(jnp.int32) + SLOTS * row_core[:, None], -1)
    slot = jnp.arange(2 * SLOTS, dtype=jnp.int32)
    filled = key.T[:, None, :] == slot[None, :, None]
    onehot = filled.reshape(experts * 2 * SLOTS, 2 * tok_dev).astype(BF16)

    height = chips * 2 * SLOTS

    def start_piece(piece, after):
        part = both[:, piece * step : (piece + 1) * step]
        if piece == 0:
            label = jnp.broadcast_to(both_tenants[:, None], (2 * tok_dev, lanes))
            part = jnp.concatenate([part, label], axis=1)
        rows = build_rows(onehot, part, after)
        got = exchange(rows.reshape(owners, 2 * SLOTS, part.shape[1]), owners)
        return got.reshape(2, height, part.shape[1])

    def spread_piece(own, after):
        from_left = over_dp(own, 1)
        from_right = over_dp(own, -1)
        lower, upper = split_halves(from_left, from_right, ())
        across = (over_dp(lower, 1), over_dp(upper, -1))
        return (own, from_left, from_right), across

    def map_part(shift):
        at = ((plane + shift) % 4) * hid_dev
        return lax.dynamic_slice_in_dim(adapter_output_maps[:, 0], at, hid_dev, axis=2)

    out_maps = jnp.concatenate(
        [
            map_part(0),
            over_dp(map_part(1), 1),
            over_dp(map_part(-1), -1),
            over_dp(map_part(2), 2),
        ],
        axis=0,
    )
    rank = rank_doubled // 2
    gate_b = out_maps[:, :rank].reshape(tenants_all * rank, hid_dev)
    up_b = out_maps[:, rank:].reshape(tenants_all * rank, hid_dev)

    maps = adapter_input_maps.reshape(own_tenants * rank_doubled, width)
    near_sums, far_sums, far, waited = (), (), (), ()
    for piece in range(PIECES):
        waited = far
        near, far = spread_piece(start_piece(piece, notes if piece == 0 else out_maps), far)
        run = functools.partial(accumulate, piece, step)
        shared = (gate_weight, up_weight, maps)
        if piece == 0:
            *near_sums, near_label = run(True, near, near_sums, *shared, True, True)
            *far_sums, far_label = run(False, far, far_sums, *shared, True, True)
        elif piece < PIECES - 1:
            near_sums = run(True, near, near_sums, *shared, True, True)
            far_sums = run(False, far, far_sums, *shared, True, True)
        else:
            near_sums = run(True, near, near_sums, *shared, True, True, after=waited)
            (far_low,) = run(False, far, far_sums[2:], *shared, False, True)
            far_acts = run(False, far, far_sums[:2], *shared, True, False)
    label_row = jnp.concatenate([near_label[:1], far_label[:1]], axis=1).astype(jnp.int32)
    low = jnp.concatenate([near_sums[2], far_low], axis=1)

    live = lax.dynamic_index_in_dim(adapter_present, owner_idx, axis=1, keepdims=False)
    own_live = lax.dynamic_slice_in_dim(live, plane * own_tenants, own_tenants)
    own_ids = plane * own_tenants + jnp.arange(own_tenants, dtype=jnp.int32)
    chosen = (label_row == own_ids[:, None]) & (own_live[:, None] != 0)
    low_own = jnp.sum(
        jnp.where(chosen[:, None, :], low.reshape(own_tenants, rank_doubled, 4 * height), 0.0),
        axis=0,
    ).astype(BF16)
    quarters = [low_own[:, i * height : (i + 1) * height] for i in range(4)]

    def arranged(order):
        return jnp.concatenate([quarters[i] for i in order], axis=1)

    low_rank = (
        low_own.astype(F32)
        + over_dp(arranged((2, 0, 3, 1)), 1).astype(F32)
        + over_dp(arranged((1, 3, 0, 2)), -1).astype(F32)
        + over_dp(arranged((3, 2, 1, 0)), 2).astype(F32)
    )
    away = (label_row // own_tenants - plane) % 4
    group = jnp.where(away == 0, 0, jnp.where(away == 3, 1, away + 1))
    label_rel = group * own_tenants + label_row % own_tenants
    split = 3 * height
    hidden_far = hidden_blocks(
        1, *far_acts, low_rank[:, split:], label_rel[:, split:], gate_b, up_b
    )
    hidden_near = hidden_blocks(
        3, *near_sums[:2], low_rank[:, :split], label_rel[:, :split], gate_b, up_b
    )

    scale = jnp.sum(jnp.where(named, both_weight[:, :, None], 0.0), axis=1)
    mix = jnp.where(filled, scale.T[:, None, :], 0.0).reshape(experts * 2 * SLOTS, 2 * tok_dev)
    mix_hi = lax.optimization_barrier(mix.astype(BF16))
    mix_lo = (mix - mix_hi.astype(F32)).astype(BF16)

    relays = [relay_blocks(piece, step, hidden_far[0], down_weight) for piece in range(PIECES)]
    relayed = [(over_dp(lower, 1), over_dp(upper, -1)) for lower, upper in relays]
    passed = [
        pass_blocks(piece, step, hidden_near[2], hidden_near[1], down_weight, *relayed[piece])
        for piece in range(PIECES)
    ]

    def return_piece(piece):
        up_sum, down_sum = passed[piece]
        after = relayed[piece + 1] if piece + 1 < PIECES else ()
        total = last_block(
            piece, step, hidden_near[0], down_weight, over_dp(up_sum, 1), over_dp(down_sum, -1), after
        )
        back = exchange(total.reshape(owners, 2 * SLOTS, step), owners)
        back = back.reshape(owners * 2 * SLOTS, step)
        contract = (((0,), (0,)), ((), ()))
        return (
            lax.dot_general(mix_hi, back, contract, preferred_element_type=F32)
            + lax.dot_general(mix_lo, back, contract, preferred_element_type=F32)
        ).astype(BF16)

    mixed = jnp.concatenate([return_piece(piece) for piece in range(PIECES)], axis=1)
    kept, sent = mixed[:tok_dev], mixed[tok_dev:]
    came = other_core(sent)
    return jnp.where(
        core == 0,
        jnp.concatenate([kept, came], axis=1),
        jnp.concatenate([came, kept], axis=1),
    )


def solution(mesh):
    placed = (
        P(("expert", "dp"), None),
        P(("expert", "dp"), None),
        P(("expert", "dp"), None),
        P(("expert", "dp")),
        P(),
        P("expert", None, "dp"),
        P("expert", None, "dp"),
        P("expert", "dp", None),
        P("dp", "expert", None, None),
        P("dp", "expert", None, None),
    )
    return jax.shard_map(
        body, mesh=mesh, in_specs=placed, out_specs=P(("expert", "dp"), None), check_vma=False
    )
```

```python
import functools

import jax
import jax.numpy as jnp
from jax import lax
from jax.experimental import pallas as pl
from jax.experimental.pallas import tpu as pltpu
from jax.sharding import PartitionSpec as P

PIECES = 2
LANES = 128
TILE = 1024
SLOTS = 4
BF16 = jnp.bfloat16
F32 = jnp.float32


def over_dp(value, shift):
    size = lax.axis_size("dp")
    return lax.ppermute(value, "dp", [(i, (i + shift) % size) for i in range(size)])


def other_core(value):
    size = lax.axis_size("expert")
    return lax.ppermute(value, "expert", [(i, i ^ 1) for i in range(size)])


def core_major(owners):
    return [list(range(0, owners, 2)) + list(range(1, owners, 2))]


def exchange(rows, owners):
    return lax.all_to_all(
        rows,
        "expert",
        split_axis=0,
        concat_axis=0,
        axis_index_groups=core_major(owners),
        tiled=True,
    )


def accumulate_kernel(first, near, with_acts, with_low, unread, *refs):
    refs = list(refs)[unread:]
    blocks = [refs.pop(0) for _ in range(3 if near else 2)]
    if with_acts:
        gate_w, up_w = refs.pop(0), refs.pop(0)
    if with_low:
        maps = refs.pop(0)
    count = 2 * with_acts + with_low
    if first:
        notes = [refs.pop(0) for _ in range(3 if near else 1)]
        label = refs.pop()
    else:
        old, refs = refs[:count], refs[count:]
    new = refs
    h = pl.program_id(0)

    @pl.when(h == 0)
    def _():
        for i in range(count):
            new[i][...] = jnp.zeros_like(new[i]) if first else old[i][...]
        if first:
            at = (lax.broadcasted_iota(jnp.int32, (8, LANES), 1) == 0).astype(BF16)
            for b, note in enumerate(notes):
                height = note.shape[1]
                label[:, pl.ds(b * height, height)] = lax.dot_general(
                    at, note[0], (((1,), (1,)), ((), ())), preferred_element_type=F32
                )

    def add(b, rows):
        height = rows.shape[0]
        span = pl.ds(b * height, height)
        if with_acts:
            new[0][span, :] += jnp.dot(rows, gate_w[0], preferred_element_type=F32)
            new[1][span, :] += jnp.dot(rows, up_w[0], preferred_element_type=F32)
        if with_low:
            new[-1][:, span] += lax.dot_general(
                maps[...], rows, (((1,), (1,)), ((), ())), preferred_element_type=F32
            )

    if near:
        for b, block in enumerate(blocks):
            add(b, block[0])
    else:
        add(0, jnp.where(h == 0, blocks[0][0], blocks[1][0]))


def accumulate(
    piece, step, near, blocks, sums, gate_weight, up_weight, maps, with_acts, with_low, after=()
):
    height = blocks[0].shape[1]
    total = (3 if near else 1) * height
    hid = gate_weight.shape[2]
    first = piece == 0
    if near:
        block_spec = pl.BlockSpec((1, height, step), lambda h: (h, 0, 0))
    else:
        block_spec = pl.BlockSpec((1, height, step), lambda h: (0, 0, 0))
    weight_spec = pl.BlockSpec((1, step, hid), lambda h: (0, h * PIECES + piece, 0))
    map_spec = pl.BlockSpec((maps.shape[0], step), lambda h: (0, h * PIECES + piece))
    operands, specs = [*after, *blocks], [block_spec] * len(blocks)
    specs = [pl.BlockSpec(memory_space=pl.ANY)] * len(after) + specs
    shapes = []
    flops = 0
    if with_acts:
        operands += [gate_weight, up_weight]
        specs += [weight_spec] * 2
        shapes += [(total, hid)] * 2
        flops += 2 * total * 2 * step * 2 * hid
    if with_low:
        operands.append(maps)
        specs.append(map_spec)
        shapes.append((maps.shape[0], total))
        flops += 2 * total * 2 * step * maps.shape[0]
    sum_specs = [pl.BlockSpec(shape, lambda h: (0, 0)) for shape in shapes]
    aliases = {}
    if first:
        noted = blocks if near else blocks[:1]
        operands += noted
        specs += [pl.BlockSpec((1, height, LANES), lambda h: (0, 0, step // LANES))] * len(noted)
        shapes.append((8, total))
        sum_specs.append(pl.BlockSpec((8, total), lambda h: (0, 0)))
    else:
        aliases = {len(operands) + i: i for i in range(len(shapes))}
        operands += list(sums)
        specs += sum_specs
    moved = 4 * total * step + sum(2 * 4 * a * b for a, b in shapes)
    return pl.pallas_call(
        functools.partial(accumulate_kernel, first, near, with_acts, with_low, len(after)),
        grid=(2,),
        in_specs=specs,
        out_specs=tuple(sum_specs),
        out_shape=tuple(jax.ShapeDtypeStruct(shape, F32) for shape in shapes),
        input_output_aliases=aliases,
        cost_estimate=pl.CostEstimate(flops=flops, bytes_accessed=moved, transcendentals=0),
        compiler_params=pltpu.CompilerParams(vmem_limit_bytes=24 * 2**20),
    )(*operands)


def hidden_kernel(gate_ref, up_ref, low_ref, tenant_ref, gate_b_ref, up_b_ref, *outs):
    low = low_ref[...]
    half = low.shape[0] // 2
    tenants = gate_b_ref.shape[0] // half
    wide = low.shape[1]
    owner = lax.broadcasted_iota(jnp.int32, (tenants * half, wide), 0) // half
    hit = owner == tenant_ref[...]
    zero = jnp.zeros((), F32)

    def spread(part):
        tall = jnp.concatenate([part] * tenants, axis=0)
        return jnp.where(hit, tall, zero).astype(BF16)

    def product(part, maps):
        return lax.dot_general(
            spread(part), maps, (((0,), (0,)), ((), ())), preferred_element_type=F32
        )

    gate = gate_ref[...] + product(low[:half], gate_b_ref[...])
    up = up_ref[...] + product(low[half:], up_b_ref[...])
    hidden = (gate / (1.0 + jnp.exp(-gate)) * up).astype(BF16)
    height = outs[0].shape[0]
    for i, out in enumerate(outs):
        out[...] = hidden[i * height : (i + 1) * height]


def hidden_blocks(count, gate, up, low, tenants, gate_b, up_b):
    total, hid = gate.shape
    shape = jax.ShapeDtypeStruct((total // count, hid), BF16)
    return pl.pallas_call(
        hidden_kernel,
        out_shape=(shape,) * count,
        cost_estimate=pl.CostEstimate(
            flops=4 * total * hid * gate_b.shape[0], bytes_accessed=9 * total * hid, transcendentals=total * hid
        ),
        compiler_params=pltpu.CompilerParams(vmem_limit_bytes=24 * 2**20),
    )(gate, up, low, tenants, gate_b, up_b)


def product(hidden, weight):
    return jnp.dot(hidden[...], weight[0], preferred_element_type=F32)


def down_cost(blocks, height, hid, step):
    return pl.CostEstimate(
        flops=4 * blocks * height * hid * step,
        bytes_accessed=6 * blocks * height * step + 4 * hid * step,
        transcendentals=0,
    )


def weight_tile(piece, step, hid):
    tiles = step // TILE
    return pl.BlockSpec(
        (1, hid, TILE), lambda h, t: (0, 0, h * PIECES * tiles + piece * tiles + t)
    )


def rows_kernel(onehot, part, after, out):
    out[...] = jnp.dot(onehot[...], part[...], preferred_element_type=F32).astype(BF16)


def build_rows(onehot, part, after):
    count, columns = onehot.shape[0], part.shape[1]
    whole = pl.BlockSpec(memory_space=pltpu.VMEM)
    return pl.pallas_call(
        rows_kernel,
        in_specs=[whole, whole, pl.BlockSpec(memory_space=pl.ANY)],
        out_specs=whole,
        out_shape=jax.ShapeDtypeStruct((count, columns), BF16),
        cost_estimate=pl.CostEstimate(
            flops=64 * count * columns, bytes_accessed=2 * count * columns, transcendentals=0
        ),
    )(onehot, part, after)


def split_kernel(left, right, *refs):
    refs[-2][...] = left[...]
    refs[-1][...] = right[...]


def split_halves(left, right, after):
    _, height, columns = left.shape
    shape = jax.ShapeDtypeStruct((1, height, columns), left.dtype)
    block = pl.BlockSpec((1, height, columns), lambda h: (0, 0, 0))
    return pl.pallas_call(
        split_kernel,
        grid=(1,),
        in_specs=[block, pl.BlockSpec((1, height, columns), lambda h: (1, 0, 0))]
        + [pl.BlockSpec(memory_space=pl.ANY)] * len(after),
        out_specs=(block, block),
        out_shape=(shape, shape),
        cost_estimate=pl.CostEstimate(
            flops=1, bytes_accessed=8 * height * columns, transcendentals=0
        ),
    )(left, right, *after)


def relay_kernel(hidden, weight, lower, upper):
    total = product(hidden, weight).astype(BF16)

    @pl.when(pl.program_id(0) == 0)
    def _():
        lower[...] = total

    @pl.when(pl.program_id(0) == 1)
    def _():
        upper[...] = total


def relay_blocks(piece, step, hidden, down_weight):
    height, hid = hidden.shape
    last = step // TILE - 1
    shape = jax.ShapeDtypeStruct((height, step), BF16)
    return pl.pallas_call(
        relay_kernel,
        grid=(2, step // TILE),
        in_specs=[
            pl.BlockSpec((height, hid), lambda h, t: (0, 0)),
            weight_tile(piece, step, hid),
        ],
        out_specs=(
            pl.BlockSpec((height, TILE), lambda h, t: (0, jnp.where(h == 0, t, last))),
            pl.BlockSpec((height, TILE), lambda h, t: (0, jnp.where(h == 0, 0, t))),
        ),
        out_shape=(shape, shape),
        cost_estimate=down_cost(1, height, hid, step),
    )(hidden, down_weight)


def pass_kernel(up_hidden, down_hidden, weight, lower, upper, up_out, down_out):
    h = pl.program_id(0)
    zero = jnp.zeros((), F32)
    up = product(up_hidden, weight) + jnp.where(h == 0, lower[...].astype(F32), zero)
    down = product(down_hidden, weight) + jnp.where(h == 1, upper[...].astype(F32), zero)
    up_out[0] = up.astype(BF16)
    down_out[0] = down.astype(BF16)


def pass_blocks(piece, step, up_hidden, down_hidden, down_weight, lower, upper):
    height, hid = up_hidden.shape
    whole = pl.BlockSpec((height, hid), lambda h, t: (0, 0))
    part = pl.BlockSpec((height, TILE), lambda h, t: (0, t))
    out = pl.BlockSpec((1, height, TILE), lambda h, t: (h, 0, t))
    shape = jax.ShapeDtypeStruct((2, height, step), BF16)
    return pl.pallas_call(
        pass_kernel,
        grid=(2, step // TILE),
        in_specs=[whole, whole, weight_tile(piece, step, hid), part, part],
        out_specs=(out, out),
        out_shape=(shape, shape),
        cost_estimate=down_cost(2, height, hid, step),
    )(up_hidden, down_hidden, down_weight, lower, upper)


def last_kernel(hidden, weight, left, right, *refs):
    total = product(hidden, weight) + left[0].astype(F32) + right[0].astype(F32)
    refs[-1][0] = total.astype(BF16)


def last_block(piece, step, hidden, down_weight, left, right, after):
    height, hid = hidden.shape
    block = pl.BlockSpec((1, height, TILE), lambda h, t: (h, 0, t))
    return pl.pallas_call(
        last_kernel,
        grid=(2, step // TILE),
        in_specs=[
            pl.BlockSpec((height, hid), lambda h, t: (0, 0)),
            weight_tile(piece, step, hid),
            block,
            block,
        ]
        + [pl.BlockSpec(memory_space=pl.ANY)] * len(after),
        out_specs=block,
        out_shape=jax.ShapeDtypeStruct((2, height, step), BF16),
        cost_estimate=down_cost(1, height, hid, step),
    )(hidden, down_weight, left, right, *after)


def body(
    tokens,
    routed_expert_index,
    routing_weight,
    token_tenant_index,
    adapter_present,
    gate_weight,
    up_weight,
    down_weight,
    adapter_input_maps,
    adapter_output_maps,
):
    owners = lax.axis_size("expert")
    chips = owners // 2
    tok_dev, width = tokens.shape
    picks = routed_expert_index.shape[1]
    tenants_all, experts = adapter_present.shape
    own_tenants, _, rank_doubled, _ = adapter_input_maps.shape
    hid_dev = gate_weight.shape[2]
    half = width // 2
    step = half // PIECES
    lanes = 128
    owner_idx = lax.axis_index("expert")
    plane = lax.axis_index("dp")
    core = owner_idx % 2

    notes = jnp.concatenate(
        [
            routed_expert_index,
            token_tenant_index[:, None],
            jnp.zeros((tok_dev, lanes - picks - 1), jnp.int32),
        ],
        axis=1,
    ).astype(BF16)
    lower, upper = tokens[:, :half], tokens[:, half:]
    mine = jnp.where(core == 0, lower, upper)
    theirs = jnp.where(core == 0, upper, lower)
    arrived = other_core(jnp.concatenate([notes, theirs], axis=1))
    both_notes = jnp.concatenate([notes, arrived[:, :lanes]], axis=0)
    both = jnp.concatenate([mine, arrived[:, lanes:]], axis=0)
    both_ids = both_notes[:, :picks].astype(jnp.int32)
    both_tenants = both_notes[:, picks]
    other_weight = other_core(routing_weight)
    both_weight = jnp.concatenate([routing_weight, other_weight], axis=0)

    place = jnp.arange(experts, dtype=jnp.int32)
    expert_order = (place % chips) * 2 + place // chips
    named = both_ids[:, :, None] == expert_order[None, None, :]
    member = jnp.any(named, axis=1)
    row = jnp.arange(2 * tok_dev, dtype=jnp.int32)
    earlier = (row[:, None] > row[None, :]) & (row[:, None] // tok_dev == row[None, :] // tok_dev)
    before = jnp.dot(earlier.astype(BF16), member.astype(BF16), preferred_element_type=F32)
    row_core = jnp.where(row < tok_dev, core, 1 - core)
    key = jnp.where(member, before.astype(jnp.int32) + SLOTS * row_core[:, None], -1)
    slot = jnp.arange(2 * SLOTS, dtype=jnp.int32)
    filled = key.T[:, None, :] == slot[None, :, None]
    onehot = filled.reshape(experts * 2 * SLOTS, 2 * tok_dev).astype(BF16)

    height = chips * 2 * SLOTS

    def start_piece(piece, after):
        part = both[:, piece * step : (piece + 1) * step]
        if piece == 0:
            label = jnp.broadcast_to(both_tenants[:, None], (2 * tok_dev, lanes))
            part = jnp.concatenate([part, label], axis=1)
        rows = build_rows(onehot, part, after)
        got = exchange(rows.reshape(owners, 2 * SLOTS, part.shape[1]), owners)
        return got.reshape(2, height, part.shape[1])

    def spread_piece(own, after):
        from_left = over_dp(own, 1)
        from_right = over_dp(own, -1)
        lower, upper = split_halves(from_left, from_right, ())
        across = (over_dp(lower, 1), over_dp(upper, -1))
        return (own, from_left, from_right), across

    def map_part(shift):
        at = ((plane + shift) % 4) * hid_dev
        return lax.dynamic_slice_in_dim(adapter_output_maps[:, 0], at, hid_dev, axis=2)

    out_maps = jnp.concatenate(
        [
            map_part(0),
            over_dp(map_part(1), 1),
            over_dp(map_part(-1), -1),
            over_dp(map_part(2), 2),
        ],
        axis=0,
    )
    rank = rank_doubled // 2
    gate_b = out_maps[:, :rank].reshape(tenants_all * rank, hid_dev)
    up_b = out_maps[:, rank:].reshape(tenants_all * rank, hid_dev)

    maps = adapter_input_maps.reshape(own_tenants * rank_doubled, width)
    near_sums, far_sums, far, waited = (), (), (), ()
    for piece in range(PIECES):
        waited = far
        near, far = spread_piece(start_piece(piece, notes if piece == 0 else out_maps), far)
        run = functools.partial(accumulate, piece, step)
        shared = (gate_weight, up_weight, maps)
        if piece == 0:
            *near_sums, near_label = run(True, near, near_sums, *shared, True, True)
            *far_sums, far_label = run(False, far, far_sums, *shared, True, True)
        elif piece < PIECES - 1:
            near_sums = run(True, near, near_sums, *shared, True, True)
            far_sums = run(False, far, far_sums, *shared, True, True)
        else:
            near_sums = run(True, near, near_sums, *shared, True, True, after=waited)
            (far_low,) = run(False, far, far_sums[2:], *shared, False, True)
            far_acts = run(False, far, far_sums[:2], *shared, True, False)
    label_row = jnp.concatenate([near_label[:1], far_label[:1]], axis=1).astype(jnp.int32)
    low = jnp.concatenate([near_sums[2], far_low], axis=1)

    live = lax.dynamic_index_in_dim(adapter_present, owner_idx, axis=1, keepdims=False)
    own_live = lax.dynamic_slice_in_dim(live, plane * own_tenants, own_tenants)
    own_ids = plane * own_tenants + jnp.arange(own_tenants, dtype=jnp.int32)
    chosen = (label_row == own_ids[:, None]) & (own_live[:, None] != 0)
    low_own = jnp.sum(
        jnp.where(chosen[:, None, :], low.reshape(own_tenants, rank_doubled, 4 * height), 0.0),
        axis=0,
    ).astype(BF16)
    quarters = [low_own[:, i * height : (i + 1) * height] for i in range(4)]

    def arranged(order):
        return jnp.concatenate([quarters[i] for i in order], axis=1)

    low_rank = (
        low_own.astype(F32)
        + over_dp(arranged((2, 0, 3, 1)), 1).astype(F32)
        + over_dp(arranged((1, 3, 0, 2)), -1).astype(F32)
        + over_dp(arranged((3, 2, 1, 0)), 2).astype(F32)
    )
    away = (label_row // own_tenants - plane) % 4
    group = jnp.where(away == 0, 0, jnp.where(away == 3, 1, away + 1))
    label_rel = group * own_tenants + label_row % own_tenants
    split = 3 * height
    hidden_far = hidden_blocks(
        1, *far_acts, low_rank[:, split:], label_rel[:, split:], gate_b, up_b
    )
    hidden_near = hidden_blocks(
        3, *near_sums[:2], low_rank[:, :split], label_rel[:, :split], gate_b, up_b
    )

    scale = jnp.sum(jnp.where(named, both_weight[:, :, None], 0.0), axis=1)
    mix = jnp.where(filled, scale.T[:, None, :], 0.0).reshape(experts * 2 * SLOTS, 2 * tok_dev)
    mix_hi = lax.optimization_barrier(mix.astype(BF16))
    mix_lo = (mix - mix_hi.astype(F32)).astype(BF16)

    relays = [relay_blocks(piece, step, hidden_far[0], down_weight) for piece in range(PIECES)]
    relayed = [(over_dp(lower, 1), over_dp(upper, -1)) for lower, upper in relays]
    passed = [
        pass_blocks(piece, step, hidden_near[2], hidden_near[1], down_weight, *relayed[piece])
        for piece in range(PIECES)
    ]

    def return_piece(piece):
        up_sum, down_sum = passed[piece]
        after = relayed[piece + 1] if piece + 1 < PIECES else ()
        total = last_block(
            piece, step, hidden_near[0], down_weight, over_dp(up_sum, 1), over_dp(down_sum, -1), after
        )
        back = exchange(total.reshape(owners, 2 * SLOTS, step), owners)
        back = back.reshape(owners * 2 * SLOTS, step)
        contract = (((0,), (0,)), ((), ()))
        return (
            lax.dot_general(mix_hi, back, contract, preferred_element_type=F32)
            + lax.dot_general(mix_lo, back, contract, preferred_element_type=F32)
        ).astype(BF16)

    mixed = jnp.concatenate([return_piece(piece) for piece in range(PIECES)], axis=1)
    kept, sent = mixed[:tok_dev], mixed[tok_dev:]
    came = other_core(sent)
    return jnp.where(
        core == 0,
        jnp.concatenate([kept, came], axis=1),
        jnp.concatenate([came, kept], axis=1),
    )


def solution(mesh):
    placed = (
        P(("expert", "dp"), None),
        P(("expert", "dp"), None),
        P(("expert", "dp"), None),
        P(("expert", "dp")),
        P(),
        P("expert", None, "dp"),
        P("expert", None, "dp"),
        P("expert", "dp", None),
        P("dp", "expert", None, None),
        P("dp", "expert", None, None),
    )
    return jax.shard_map(
        body, mesh=mesh, in_specs=placed, out_specs=P(("expert", "dp"), None), check_vma=False
    )
```
